256 devices in a mesh: tile: 64 (over y, z_hi, x, core), plane: 4 (over z_lo).
Axes of the slice: x: 4, y: 4, z: 8 (z_hi: 2, z_lo: 4; z = z_hi * 4 + z_lo), core: 2. Of those that a mesh axis runs over, the one named last changes fastest.
Arguments:
- raw_tiles: bfloat16 [4, 512, 2, 16, 1024], P('plane', 'tile'), may hold values from 0.5 to 2.5
- flat_profile: bfloat16 [2, 16, 1024], P(None, 'plane'), may hold values from 0.5 to 1.5
- dark_profile: bfloat16 [2, 16, 1024], P(None, 'plane'), may hold values from 0 to 0.5
- destinations: int32 [4, 512, 1], P('plane', 'tile'), may hold values from 0 to 63, as said below
- positions: int32 [4, 512], P('plane', 'tile'), may hold values from 0 to 31
- levels: int32 [4, 512], P('plane', 'tile'), may hold values from 1 to 4
Outputs:
- stitched: bfloat16 [4, 2, 32768, 1024], P('plane', None, 'tile')
The draws below stay inside these ranges and needn't reach their ends.
Inputs may be any that keep to these rules, and one draw needn't show every extreme that they name: `destinations`: the owner of a tile acquired by the device at index i of tile (aligned blocks of 8 tiles of a plane) is one of i - 2, ..., i + 2 or i + 32, modulo 64; among one device's tiles no owner is named more than 2 times, some owner exactly 2 times, and the owner i + 32 exactly 2 times.
All inputs are finite; a program needn't handle non-finite values.
Results may differ from the reference program's by a relative error of at most 0.0045.
Values may be sent and summed in bfloat16 or wider, within the bound.
A program may use at most 64 MiB of HBM per device.

```python
import jax
import jax.numpy as jnp
from jax import lax

W = 1024
CH = 2
TR = 16
CR = 512
NT = 8
CAP = 2
PLANES = 4
TILES = 512
N_TILE = 64
N_PLANE = 4


def draw_destinations(key, part):
    block_total = PLANES * N_TILE

    def one_block(block_key, block_id):
        key_full, key_mix, key_final = jax.random.split(block_key, 3)
        full_offset = jax.random.randint(key_full, (), 0, 5)
        base = jnp.repeat(jnp.arange(6, dtype=jnp.int32), CAP)
        mixed = base[jax.random.permutation(key_mix, 6 * CAP)]
        rank_key = jnp.where(mixed == full_offset, 0, jnp.where(mixed == 5, 1, 2)).astype(jnp.int32)
        order = jnp.argsort(rank_key, stable=True)
        chosen = mixed[order][:NT]
        chosen = jax.random.permutation(key_final, chosen)
        device_id = block_id % N_TILE
        step_to = jnp.where(chosen == 5, N_TILE // 2, chosen - 2)
        return ((device_id + step_to) % N_TILE).astype(jnp.int32)
    block_keys = jax.random.split(jax.random.fold_in(key, 71), block_total)
    owners = jax.vmap(one_block)(block_keys, jnp.arange(block_total, dtype=jnp.int32))
    return owners.reshape(PLANES, N_TILE * NT, 1).astype(jnp.int32)


def place_ends(entries, rng, smallest, largest):
    shape = entries.shape
    index_at = [jax.random.randint(jax.random.fold_in(rng, axis), (), 0, shape[axis]) for axis in range(len(shape))]
    entries = entries.at[tuple(index_at)].set(smallest)
    longest = shape.index(max(shape))
    index_at[longest] = (index_at[longest] + 1) % shape[longest]
    return entries.at[tuple(index_at)].set(largest)


def block_levels(rng, extent, cuts, low, largest):
    loudness = 1.0
    for position, shards_of in cuts:
        draws = jax.random.uniform(jax.random.fold_in(jax.random.fold_in(rng, 6), position), (shards_of,), jnp.float32, low / len(cuts), largest / len(cuts))
        loudness = loudness * jnp.repeat(jnp.exp(draws), extent[position] // shards_of).reshape((-1,) + (1,) * (len(extent) - 1 - position))
    return loudness


def setup_inputs(seed: int = 0) -> dict:
    arg_keys = jax.random.split(jax.random.key(seed), 7)
    raw_tiles = jnp.clip(0.5 + 2.0 * jax.random.uniform(arg_keys[0], (PLANES, TILES, CH, TR, W), jnp.float32) ** block_levels(arg_keys[0], (PLANES, TILES, CH, TR, W), ((0, 4), (1, 64)), -0.2, 0.2), 0.5, 2.5).astype(jnp.bfloat16)
    flat_profile = jnp.clip(0.5 + 1.0 * jax.random.uniform(arg_keys[1], (CH, TR, W), jnp.float32) ** block_levels(arg_keys[1], (CH, TR, W), ((1, 4),), -0.2, 0.2), 0.5, 1.5).astype(jnp.bfloat16)
    dark_profile = jnp.clip(0.5 * jax.random.uniform(arg_keys[2], (CH, TR, W), jnp.float32) ** block_levels(arg_keys[2], (CH, TR, W), ((1, 4),), -0.2, 0.2), 0.0, 0.5).astype(jnp.bfloat16)
    destinations = draw_destinations(jax.random.fold_in(arg_keys[6], 71), 0)
    positions = place_ends(jax.random.randint(arg_keys[4], (PLANES, TILES), 0, (CR - TR) // 16 + 1), jax.random.fold_in(arg_keys[4], 1), 0, ((CR - TR) // 16 + 1) - 1).astype(jnp.int32)
    levels = place_ends(jax.random.randint(arg_keys[5], (PLANES, TILES), 1, 5), jax.random.fold_in(arg_keys[5], 1), 1, 4).astype(jnp.int32)
    return {"raw_tiles": raw_tiles, "flat_profile": flat_profile, "dark_profile": dark_profile, "destinations": destinations, "positions": positions, "levels": levels}


screen_weight = 0.5


def ramp_weights():
    tile_row = jnp.arange(TR)
    return jnp.minimum(tile_row + 1, TR - tile_row).astype(jnp.float32)


def apply_weights(camera, flat_full, dark_full, gains):
    corrected = (camera.astype(jnp.float32) - dark_full.astype(jnp.float32)) / flat_full.astype(jnp.float32)
    scale = gains * ramp_weights()[:, None]
    return (corrected * scale).astype(jnp.bfloat16)


def smooth_sweep(field, blended):
    padded = jnp.pad(field, ((0, 0), (1, 1), (1, 1)))
    neighbours = padded[:, :-2, 1:-1] + padded[:, 2:, 1:-1] + padded[:, 1:-1, :-2] + padded[:, 1:-1, 2:]
    return (screen_weight * blended + neighbours) / (screen_weight + 4.0)


def stitch_plane(camera, owners, grid_pos, gains, flat_profile, dark_profile):
    anchor = jnp.zeros((), jnp.int32)

    def add_tile(state_pair, record):
        accumulated, weight_sum = state_pair
        one_tile, owner, offset, gain = record
        first_row = (owner * CR + 16 * offset).astype(jnp.int32)
        weighted = apply_weights(one_tile, flat_profile, dark_profile, gain.astype(jnp.float32)).astype(jnp.float32)
        current = lax.dynamic_slice(accumulated, (anchor, first_row, anchor), (CH, TR, W))
        accumulated = lax.dynamic_update_slice(accumulated, current + weighted, (anchor, first_row, anchor))
        current_w = lax.dynamic_slice(weight_sum, (first_row,), (TR,))
        weight_sum = lax.dynamic_update_slice(weight_sum, current_w + gain.astype(jnp.float32) * ramp_weights(), (first_row,))
        return (accumulated, weight_sum), None

    start_pair = (jnp.zeros((CH, N_TILE * CR, W), jnp.float32), jnp.zeros((N_TILE * CR,), jnp.float32))
    (accumulated, weight_sum), _ = lax.scan(add_tile, start_pair, (camera, owners[:, 0], grid_pos, gains))
    blended = accumulated / jnp.maximum(weight_sum, 1.0)[None, :, None]
    field = blended
    for sweep_id in range(3):
        field = smooth_sweep(field, blended)
    return field.astype(jnp.bfloat16)


def reference(raw_tiles, flat_profile, dark_profile, destinations, positions, levels):
    planes_out = []
    for plane_id in range(N_PLANE):
        planes_out.append(stitch_plane(raw_tiles[plane_id], destinations[plane_id], positions[plane_id], levels[plane_id], flat_profile, dark_profile))
    return jnp.stack(planes_out, 0)
```

```python
import functools

import jax
import jax.numpy as jnp
from jax import lax
from jax.experimental import pallas as pl
from jax.experimental.pallas import tpu as pltpu
from jax.sharding import PartitionSpec as P

MESH = pl.DeviceIdType.MESH
F32 = jnp.float32
BF16 = jnp.bfloat16
OWNER_ROWS = 512
TILE_ROWS = 16
NEAR = (-2, -1, 1, 2)
GROUPS = 7
DEPTH = GROUPS * 128
Q = 1.0 / 4.5
Q2 = Q * Q
Q3 = Q2 * Q


def stitch_kernel(
    n_tile, n_plane, width,
    dest_ref, pos_ref, level_ref, raw_ref, flat_ref, dark_ref, out_ref,
    rawv, sbuf, rbuf, smeta, rmeta, prof, dark_v, inv_v, pos_all, gain_all, g_all,
    edge, strip, sblk, rblk, sstrip, rstrip, vbuf, mbuf, obuf,
    raw_sem, own_sem, out_sem,
    tile_s, tile_r, meta_s, meta_r, gat_s, gat_r, swap_s, swap_r, blk_s, blk_r, str_s, str_r,
):
    me = lax.axis_index("tile")
    plane = lax.axis_index("plane")
    core = lax.rem(me, 2)
    column = lax.rem(me // 2, 4)
    up = column >= 2
    half = n_tile // 2
    reps = width // 128

    def at(offset):
        return {"tile": lax.rem(me + offset + n_tile, n_tile), "plane": plane}

    load_raw = pltpu.make_async_copy(raw_ref.at[0], rawv, raw_sem)
    load_raw.start()

    @pl.when(core == 0)
    def _():
        pltpu.make_async_copy(flat_ref, prof.at[0, plane], own_sem).start()

    @pl.when(core == 1)
    def _():
        pltpu.make_async_copy(dark_ref, prof.at[1, plane], own_sem).start()

    barrier = pltpu.get_barrier_semaphore()
    for offset in NEAR + (half,):
        pl.semaphore_signal(barrier, inc=1, device_id=at(offset), device_id_type=MESH)
    for k in range(1, n_plane):
        mate = {"tile": me, "plane": lax.rem(plane + k, n_plane)}
        pl.semaphore_signal(barrier, inc=1, device_id=mate, device_id_type=MESH)

    rel = [lax.rem(dest_ref[0, t, 0] - me + 2 + 2 * n_tile, n_tile) for t in range(8)]
    load_raw.wait()
    for e, offset in enumerate(NEAR + (half, 0)):
        key = offset + 2
        first, last, hits = jnp.int32(0), jnp.int32(0), jnp.int32(0)
        for t in range(8):
            hit = rel[t] == key
            last = jnp.where(hit, t, last)
            hits = hits + jnp.where(hit, 1, 0)
            first = jnp.where(rel[7 - t] == key, 7 - t, first)
        gain0 = jnp.where(hits > 0, level_ref[0, first], 0).astype(F32)
        gain1 = jnp.where(hits > 1, level_ref[0, last], 0).astype(F32)
        pos0 = pos_ref[0, first].astype(F32)
        pos1 = pos_ref[0, last].astype(F32)
        row = lax.broadcasted_iota(jnp.int32, (8, 128), 0)
        meta = jnp.where(row == 0, pos0, jnp.where(row == 1, pos1, jnp.where(row == 2, gain0, gain1)))
        smeta[e] = meta
        if e == 5:
            rmeta[5] = meta
            rbuf[5, 0] = rawv[first]
            rbuf[5, 1] = rawv[last]
        else:
            sbuf[e, 0] = rawv[first]
            sbuf[e, 1] = rawv[last]

    def profile_wait_own():
        pltpu.make_async_copy(flat_ref, prof.at[core, plane], own_sem).wait()

    profile_wait_own()
    pl.semaphore_wait(barrier, 4 + n_plane)

    sends = []

    def send(src, dst, s_sem, r_sem, device):
        copy = pltpu.make_async_remote_copy(src, dst, s_sem, r_sem, device_id=device, device_id_type=MESH)
        copy.start()
        sends.append(copy)

    def slot_at_target(e):
        return 3 - e if e < 4 else 4

    for e, offset in enumerate(NEAR + (half,)):
        f = slot_at_target(e)
        send(smeta.at[e], rmeta.at[f], meta_s.at[e], meta_r.at[f], at(offset))
    for j in range(2):
        e = jnp.where(up, 3 - j, j)
        offset = jnp.where(up, 2 - j, j - 2)
        for k in range(2):
            send(sbuf.at[e, k], rbuf.at[3 - e, k], tile_s.at[e, k], tile_r.at[3 - e, k], at(offset))
    for k in range(1, n_plane):
        mate = {"tile": me, "plane": lax.rem(plane + k, n_plane)}
        send(prof.at[core, plane], prof.at[core, plane], gat_s.at[k], gat_r.at[plane], mate)
    for k in range(2):
        send(sbuf.at[4, k], rbuf.at[4, k], tile_s.at[4, k], tile_r.at[4, k], at(half))
    for j in range(2):
        e = jnp.where(up, j, 3 - j)
        offset = jnp.where(up, j - 2, 2 - j)
        for k in range(2):
            send(sbuf.at[e, k], rbuf.at[3 - e, k], tile_s.at[e, k], tile_r.at[3 - e, k], at(offset))

    for k in range(1, n_plane):
        source = lax.rem(plane + k, n_plane)
        pltpu.make_async_remote_copy(
            prof.at[core, source], prof.at[core, source], gat_s.at[k], gat_r.at[source],
            device_id=at(1), device_id_type=MESH,
        ).wait_recv()
    other = {"tile": me + 1 - 2 * core, "plane": plane}
    send(prof.at[core], prof.at[core], swap_s, swap_r, other)
    pltpu.make_async_remote_copy(
        prof.at[1 - core], prof.at[1 - core], swap_s, swap_r, device_id=other, device_id_type=MESH
    ).wait_recv()
    part = TILE_ROWS // n_plane
    for p in range(n_plane):
        inv_v[:, p * part:(p + 1) * part, :] = 1.0 / prof[0, p].astype(F32)
        dark_v[:, p * part:(p + 1) * part, :] = prof[1, p].astype(F32)

    row16 = lax.broadcasted_iota(jnp.int32, (TILE_ROWS, 128), 0)
    ramp = jnp.minimum(row16 + 1, TILE_ROWS - row16).astype(F32)

    def wide(x):
        return jnp.concatenate([x] * reps, axis=1)

    for e in range(4):
        lo, at_pos = (8, 31.0) if e < 2 else (0, 0.0)
        for ch in range(2):
            total = None
            for k in range(2):
                keep = jnp.where(smeta[e, k:k + 1, :] == at_pos, 1.0, 0.0)
                scale = wide(ramp[lo:lo + 8] * smeta[e, 2 + k:3 + k, :])
                tile = sbuf[e, k, ch].astype(F32)[lo:lo + 8]
                w = (tile - dark_v[ch, lo:lo + 8]) * inv_v[ch, lo:lo + 8] * scale
                w = w.astype(BF16).astype(F32) * wide(jnp.broadcast_to(keep, (8, 128)))
                total = w if total is None else total + w
            strip[e, ch] = total
    for j, (e, offset) in enumerate(((0, -1), (3, 1))):
        sstrip[j] = jnp.concatenate([strip[e, 0], strip[e, 1]], axis=0).astype(BF16)
        send(sstrip.at[j], rstrip.at[1 - j], str_s.at[j], str_r.at[1 - j], at(offset))

    order = (5, 4) + tuple(jnp.where(up, a, 3 - a) for a in (1, 0, 2, 3))
    for f in range(5):
        pltpu.make_async_remote_copy(
            smeta.at[f], rmeta.at[f], meta_s.at[f], meta_r.at[f], device_id=at(1), device_id_type=MESH
        ).wait_recv()
    pos_all[...] = jnp.full((16, 128), -99.0, F32)
    gain_all[...] = jnp.zeros((16, 128), F32)
    for m in range(6):
        pos_all[2 * m:2 * m + 2] = rmeta[order[m], 0:2]
        gain_all[2 * m:2 * m + 2] = rmeta[order[m], 2:4]
    positions, gains = pos_all[...], gain_all[...]

    def gain_sum(p):
        return jnp.sum(jnp.where(positions == p, gains, 0.0), axis=0, keepdims=True)

    for j in range(12):
        g_all[j:j + 1] = gain_sum(positions[j:j + 1])
    gain_first, gain_last = gain_sum(0.0), gain_sum(31.0)

    lane = lax.broadcasted_iota(jnp.int32, (1, 128), 1)
    gap = lax.rem(lane // TILE_ROWS, 4).astype(F32)
    y = lax.broadcasted_iota(jnp.int32, (OWNER_ROWS, 128), 0).astype(F32)
    top_shift = jnp.where(me == 0, 2.0, 1e6).astype(F32)
    bottom_shift = jnp.where(me == n_tile - 1, -2.0 * OWNER_ROWS, 1e6).astype(F32)
    for m in range(GROUPS):
        if m < 6:
            p0, p1 = positions[2 * m:2 * m + 1], positions[2 * m + 1:2 * m + 2]
        else:
            p0, p1 = -1.0, float(OWNER_ROWS // TILE_ROWS)
        source_row = jnp.where(lane < 64, p0, p1) * TILE_ROWS + lax.rem(lane, TILE_ROWS).astype(F32)
        hit = jnp.where(jnp.abs(y - source_row) == gap, 1.0, 0.0)
        above = jnp.where(jnp.abs(y + source_row + top_shift) == gap, 1.0, 0.0)
        below = jnp.where(jnp.abs(y + source_row + bottom_shift) == gap, 1.0, 0.0)
        mbuf[:, m * 128:(m + 1) * 128] = (hit - above - below).astype(BF16)

    col = lax.broadcasted_iota(jnp.int32, (TILE_ROWS, width), 1)
    not_first, not_last = col > 0, col < width - 1

    def sides(x):
        return jnp.where(not_first, pltpu.roll(x, 1, 1), 0.0) + jnp.where(
            not_last, pltpu.roll(x, width - 1, 1), 0.0
        )

    def spread(m, k, ch, b):
        c1 = sides(b)
        c2 = sides(c1)
        c3 = sides(c2)
        two = (0.5 * Q3) * b + (3.0 * Q3) * c1
        zero = (0.5 * Q) * b + (0.5 * Q2) * c1 + (0.5 * Q3) * c2 + Q3 * c3 + 2.0 * two
        one = (0.5 * Q2 + 3.0 * Q3) * b + Q3 * c1 + (3.0 * Q3) * c2
        base = m * 128 + k * 64
        for d, v in enumerate((zero, one, two, Q3 * b)):
            start = base + d * TILE_ROWS
            if not isinstance(start, int):
                start = pl.multiple_of(start, TILE_ROWS)
            vbuf[ch, pl.ds(start, TILE_ROWS), :] = v.astype(BF16)

    edge[...] = jnp.zeros(edge.shape, F32)
    last_row = jnp.where(up, 31.0, 0.0).astype(F32)
    other_row = jnp.where(up, 0.0, 31.0).astype(F32)

    def work(m):
        e = order[m]
        if m > 0:
            for k in range(2):
                pltpu.make_async_remote_copy(
                    sbuf.at[0, k], rbuf.at[e, k], tile_s.at[0, k], tile_r.at[e, k],
                    device_id=at(1), device_id_type=MESH,
                ).wait_recv()

        def unit(u, carry):
            k, ch = u // 2, lax.rem(u, 2)
            gain = gain_all[pl.ds(2 * m + k, 1), :]
            p = pos_all[pl.ds(2 * m + k, 1), :]
            g = g_all[pl.ds(2 * m + k, 1), :]
            w = (rbuf[e, k, ch].astype(F32) - dark_v[ch]) * inv_v[ch] * wide(ramp * gain)
            w = w.astype(BF16).astype(F32)
            lower, upper = w[0:8], w[8:16]
            if m < 4:
                keep = wide(jnp.broadcast_to(jnp.where(p == last_row, 1.0, 0.0), (8, 128)))
                edge[0, ch] += keep * jnp.where(up, upper, lower)
            if m < 2 or m >= 4:
                keep = wide(jnp.broadcast_to(jnp.where(p == other_row, 1.0, 0.0), (8, 128)))
                edge[1, ch] += keep * jnp.where(up, lower, upper)
            spread(m, k, ch, w * wide(1.0 / jnp.maximum(ramp * g, 1.0)))
            return carry

        lax.fori_loop(0, 4, unit, 0)

    def send_edge(j):
        down = up if j == 0 else jnp.logical_not(up)
        total = jnp.where(down, gain_last, gain_first)
        mark = lax.broadcasted_iota(jnp.int32, (8, width), 0) == 4
        block = [jnp.where(mark, wide(jnp.broadcast_to(total, (8, 128))), edge[j, ch]) for ch in range(2)]
        sblk[j] = jnp.concatenate(block, axis=0).astype(BF16)
        offset = jnp.where(down, 1, -1)
        lands = jnp.where(down, 0, 1)
        send(sblk.at[j], rblk.at[lands], blk_s.at[j], blk_r.at[lands], at(offset))

    for m in range(4):
        work(m)
    send_edge(0)
    for m in range(4, 6):
        work(m)
    send_edge(1)

    for j in range(2):
        pltpu.make_async_remote_copy(
            sstrip.at[j], rstrip.at[j], str_s.at[j], str_r.at[j], device_id=at(1), device_id_type=MESH
        ).wait_recv()
        pltpu.make_async_remote_copy(
            sblk.at[j], rblk.at[j], blk_s.at[j], blk_r.at[j], device_id=at(1), device_id_type=MESH
        ).wait_recv()
    for j in range(2):
        inside = jnp.where(me == (0 if j == 0 else n_tile - 1), 0.0, 1.0).astype(F32)
        lo = 8 - 8 * j
        got, direct = rblk[j].astype(F32), rstrip[1 - j].astype(F32)
        weights = jnp.broadcast_to(got[4:5], (8, width)) * wide(ramp[lo:lo + 8])
        scale = inside / jnp.maximum(weights, 1.0)
        for ch in range(2):
            rows = (got[8 * ch:8 * ch + 8] + direct[8 * ch:8 * ch + 8] + strip[1 + j, ch]) * scale
            none = jnp.zeros((8, width), F32)
            spread(6, j, ch, jnp.concatenate([none, rows] if j == 0 else [rows, none], axis=0))

    span = 256

    def block(n, carry):
        ch, start = n // (width // span), pl.multiple_of(lax.rem(n, width // span) * span, span)
        made = jnp.dot(mbuf[...], vbuf[ch, :, pl.ds(start, span)], preferred_element_type=F32)
        obuf[ch, :, pl.ds(start, span)] = made.astype(BF16)
        pltpu.make_async_copy(
            obuf.at[ch, :, pl.ds(start, span)], out_ref.at[0, ch, :, pl.ds(start, span)], out_sem.at[n]
        ).start()
        return carry

    blocks = 2 * width // span
    lax.fori_loop(0, blocks, block, 0)
    for n in range(blocks):
        ch, start = n // (width // span), n % (width // span) * span
        pltpu.make_async_copy(
            obuf.at[ch, :, pl.ds(start, span)], out_ref.at[0, ch, :, pl.ds(start, span)], out_sem.at[n]
        ).wait()
    for copy in sends:
        copy.wait_send()


def solution(mesh):
    n_tile, n_plane = mesh.shape["tile"], mesh.shape["plane"]

    def per_device(raw_tiles, flat_profile, dark_profile, destinations, positions, levels):
        width = raw_tiles.shape[-1]
        tile = (2, TILE_ROWS, width)
        dma = pltpu.SemaphoreType.DMA
        return pl.pallas_call(
            functools.partial(stitch_kernel, n_tile, n_plane, width),
            out_shape=jax.ShapeDtypeStruct((1, 2, OWNER_ROWS, width), BF16),
            in_specs=[pl.BlockSpec(memory_space=pltpu.SMEM)] * 3 + [pl.BlockSpec(memory_space=pl.ANY)] * 3,
            out_specs=pl.BlockSpec(memory_space=pl.ANY),
            scratch_shapes=[
                pltpu.VMEM((8,) + tile, BF16),
                pltpu.VMEM((5, 2) + tile, BF16),
                pltpu.VMEM((6, 2) + tile, BF16),
                pltpu.VMEM((6, 8, 128), F32),
                pltpu.VMEM((6, 8, 128), F32),
                pltpu.VMEM((2, n_plane, 2, TILE_ROWS // n_plane, width), BF16),
                pltpu.VMEM(tile, F32),
                pltpu.VMEM(tile, F32),
                pltpu.VMEM((16, 128), F32),
                pltpu.VMEM((16, 128), F32),
                pltpu.VMEM((16, 128), F32),
                pltpu.VMEM((2, 2, 8, width), F32),
                pltpu.VMEM((4, 2, 8, width), F32),
                pltpu.VMEM((2, 16, width), BF16),
                pltpu.VMEM((2, 16, width), BF16),
                pltpu.VMEM((2, 16, width), BF16),
                pltpu.VMEM((2, 16, width), BF16),
                pltpu.VMEM((2, DEPTH, width), BF16),
                pltpu.VMEM((OWNER_ROWS, DEPTH), BF16),
                pltpu.VMEM((2, OWNER_ROWS, width), BF16),
                dma, dma, dma((2 * width // 256,)),
                dma((5, 2)), dma((5, 2)), dma((5,)), dma((5,)),
                dma((n_plane,)), dma((n_plane,)), dma, dma,
                dma((2,)), dma((2,)), dma((2,)), dma((2,)),
            ],
            compiler_params=pltpu.CompilerParams(
                collective_id=0, has_side_effects=True, vmem_limit_bytes=48 << 20
            ),
            name="stitch",
        )(destinations, positions, levels, raw_tiles, flat_profile, dark_profile)

    placed = (
        P("plane", "tile", None, None, None),
        P(None, "plane", None),
        P(None, "plane", None),
        P("plane", "tile", None),
        P("plane", "tile"),
        P("plane", "tile"),
    )
    return jax.shard_map(
        per_device, mesh=mesh, in_specs=placed, out_specs=P("plane", None, "tile", None), check_vma=False
    )
```

```python
import functools

import jax
import jax.numpy as jnp
from jax import lax
from jax.experimental import pallas as pl
from jax.experimental.pallas import tpu as pltpu
from jax.sharding import PartitionSpec as P

MESH = pl.DeviceIdType.MESH
F32 = jnp.float32
BF16 = jnp.bfloat16
OWNER_ROWS = 512
TILE_ROWS = 16
NEAR = (-2, -1, 1, 2)
GROUPS = 6
DEPTH = GROUPS * 128
NEARER = 4 * 128
SPAN = 256
Q = 1.0 / 4.5
Q2 = Q * Q
Q3 = Q2 * Q


def stitch_kernel(
    n_tile, n_plane, width,
    dest_hbm, pos_hbm, level_hbm, raw_ref, flat_ref, dark_ref, out_ref,
    dest_ref, pos_ref, level_ref,
    rawv, sbuf, rbuf, smeta, rmeta, prof, dark_v, inv_v, pos_all, gain_all, g_all,
    edge, strip, sblk, rblk, sstrip, rstrip, vbuf, mbuf, acc, rim, vrim, mrim,
    raw_sem, own_sem, int_sem,
    tile_s, tile_r, meta_s, meta_r, gat_s, gat_r, side_s, side_r, swap_s, swap_r, blk_s, blk_r, str_s, str_r,
):
    me = lax.axis_index("tile")
    plane = lax.axis_index("plane")
    core = lax.rem(me, 2)
    column = lax.rem(me // 2, 4)
    up = column >= 2
    inner = jnp.logical_or(column == 1, column == 2)
    half = n_tile // 2
    reps = width // 128

    def at(offset):
        return {"tile": lax.rem(me + offset + n_tile, n_tile), "plane": plane}

    def mate(k):
        return {"tile": me, "plane": lax.rem(plane + k, n_plane)}

    barrier = pltpu.get_barrier_semaphore()
    for offset in NEAR + (half,):
        pl.semaphore_signal(barrier, inc=1, device_id=at(offset), device_id_type=MESH)

    @pl.when(inner)
    def _():
        for k in range(1, n_plane):
            pl.semaphore_signal(barrier, inc=1, device_id=mate(k), device_id_type=MESH)

    loads = [
        pltpu.make_async_copy(src, dst, int_sem.at[j])
        for j, (src, dst) in enumerate(((dest_hbm, dest_ref), (pos_hbm, pos_ref), (level_hbm, level_ref)))
    ]
    for load in loads:
        load.start()
    load_raw = pltpu.make_async_copy(raw_ref.at[0], rawv, raw_sem)
    load_raw.start()

    @pl.when(jnp.logical_and(inner, core == 0))
    def _():
        pltpu.make_async_copy(flat_ref, prof.at[0, plane], own_sem).start()

    @pl.when(jnp.logical_and(inner, core == 1))
    def _():
        pltpu.make_async_copy(dark_ref, prof.at[1, plane], own_sem).start()

    for load in loads:
        load.wait()
    rel = [lax.rem(dest_ref[0, t] - me + 2 + 2 * n_tile, n_tile) for t in range(8)]
    picks = []
    for e, offset in enumerate(NEAR + (half, 0)):
        key = offset + 2
        first, last, hits = jnp.int32(0), jnp.int32(0), jnp.int32(0)
        for t in range(8):
            hit = rel[t] == key
            last = jnp.where(hit, t, last)
            hits = hits + jnp.where(hit, 1, 0)
            first = jnp.where(rel[7 - t] == key, 7 - t, first)
        gain0 = jnp.where(hits > 0, level_ref[0, first], 0).astype(F32)
        gain1 = jnp.where(hits > 1, level_ref[0, last], 0).astype(F32)
        pos0 = pos_ref[0, first].astype(F32)
        pos1 = pos_ref[0, last].astype(F32)
        row = lax.broadcasted_iota(jnp.int32, (8, 128), 0)
        meta = jnp.where(row == 0, pos0, jnp.where(row == 1, pos1, jnp.where(row == 2, gain0, gain1)))
        smeta[e] = meta
        if e == 5:
            rmeta[5] = meta
        picks.append((first, last))
    load_raw.wait()
    for e, (first, last) in enumerate(picks):
        if e == 5:
            rbuf[5, 0] = rawv[first]
            rbuf[5, 1] = rawv[last]
        else:
            sbuf[e, 0] = rawv[first]
            sbuf[e, 1] = rawv[last]

    @pl.when(inner)
    def _():
        pltpu.make_async_copy(flat_ref, prof.at[core, plane], own_sem).wait()
        pl.semaphore_wait(barrier, 4 + n_plane)

    @pl.when(jnp.logical_not(inner))
    def _():
        pl.semaphore_wait(barrier, 5)

    sends = []

    def remote(src, dst, s_sem, r_sem, device):
        return pltpu.make_async_remote_copy(src, dst, s_sem, r_sem, device_id=device, device_id_type=MESH)

    def send(src, dst, s_sem, r_sem, device):
        copy = remote(src, dst, s_sem, r_sem, device)
        copy.start()
        sends.append(copy)

    def slot_at_target(e):
        return 3 - e if e < 4 else 4

    for e, offset in enumerate(NEAR + (half,)):
        f = slot_at_target(e)
        send(smeta.at[e], rmeta.at[f], meta_s.at[e], meta_r.at[f], at(offset))

    @pl.when(inner)
    def _():
        for k in range(1, n_plane):
            remote(prof.at[core, plane], prof.at[core, plane], gat_s.at[k], gat_r.at[plane], mate(k)).start()

    for j in range(2):
        e = jnp.where(up, 3 - j, j)
        offset = jnp.where(up, 2 - j, j - 2)
        for k in range(2):
            send(sbuf.at[e, k], rbuf.at[3 - e, k], tile_s.at[e, k], tile_r.at[3 - e, k], at(offset))
    for k in range(2):
        send(sbuf.at[4, k], rbuf.at[4, k], tile_s.at[4, k], tile_r.at[4, k], at(half))
    for j in range(2):
        e = jnp.where(up, j, 3 - j)
        offset = jnp.where(up, j - 2, 2 - j)
        for k in range(2):
            send(sbuf.at[e, k], rbuf.at[3 - e, k], tile_s.at[e, k], tile_r.at[3 - e, k], at(offset))

    beside = at(jnp.where(up, 2, -2))
    to_side = remote(prof.at[core], prof.at[core], side_s, side_r, beside)

    @pl.when(inner)
    def _():
        for k in range(1, n_plane):
            source = lax.rem(plane + k, n_plane)
            remote(prof.at[core, source], prof.at[core, source], gat_s.at[k], gat_r.at[source], mate(k)).wait_recv()
        to_side.start()

    @pl.when(jnp.logical_not(inner))
    def _():
        to_side.wait_recv()

    other = {"tile": me + 1 - 2 * core, "plane": plane}
    send(prof.at[core], prof.at[core], swap_s, swap_r, other)

    row16 = lax.broadcasted_iota(jnp.int32, (TILE_ROWS, 128), 0)
    ramp = jnp.minimum(row16 + 1, TILE_ROWS - row16).astype(F32)
    lane = lax.broadcasted_iota(jnp.int32, (1, 128), 1)
    gap = lax.rem(lane // TILE_ROWS, 4).astype(F32)
    lane_row = lax.rem(lane, TILE_ROWS).astype(F32)
    lane16 = lax.broadcasted_iota(jnp.int32, (TILE_ROWS, 128), 1)
    is_first, is_last = lane16 == 0, lane16 == 127

    def wide(x):
        return jnp.concatenate([x] * reps, axis=1)

    y32 = lax.broadcasted_iota(jnp.int32, (32, 128), 0)
    y32 = jnp.where(y32 < 16, y32, y32 + OWNER_ROWS - 32).astype(F32)
    rim_row = jnp.where(lane_row < 8, lane_row + OWNER_ROWS, lane_row - 16.0)
    mrim[...] = jnp.where(jnp.abs(y32 - rim_row) == gap, 1.0, 0.0).astype(BF16)[:, 0:64]
    edge[...] = jnp.zeros(edge.shape, F32)
    pos_all[...] = jnp.full((16, 128), -99.0, F32)
    gain_all[...] = jnp.zeros((16, 128), F32)

    remote(prof.at[1 - core], prof.at[1 - core], swap_s, swap_r, other).wait_recv()
    part = TILE_ROWS // n_plane
    for p in range(n_plane):
        inv_v[:, p * part:(p + 1) * part, :] = 1.0 / prof[0, p].astype(F32)
        dark_v[:, p * part:(p + 1) * part, :] = prof[1, p].astype(F32)

    for e in range(4):
        lo, at_pos = (8, 31.0) if e < 2 else (0, 0.0)
        for ch in range(2):
            total = None
            for k in range(2):
                keep = jnp.where(smeta[e, k:k + 1, :] == at_pos, 1.0, 0.0)
                scale = wide(ramp[lo:lo + 8] * smeta[e, 2 + k:3 + k, :])
                tile = sbuf[e, k, ch].astype(F32)[lo:lo + 8]
                w = (tile - dark_v[ch, lo:lo + 8]) * inv_v[ch, lo:lo + 8] * scale
                w = w.astype(BF16).astype(F32) * wide(jnp.broadcast_to(keep, (8, 128)))
                total = w if total is None else total + w
            strip[e, ch] = total
    for j, (e, offset) in enumerate(((0, -1), (3, 1))):
        sstrip[j] = jnp.concatenate([strip[e, 0], strip[e, 1]], axis=0).astype(BF16)
        send(sstrip.at[j], rstrip.at[1 - j], str_s.at[j], str_r.at[1 - j], at(offset))

    order = (5, 4) + tuple(jnp.where(up, a, 3 - a) for a in (1, 0, 2, 3))
    for f in range(5):
        remote(smeta.at[f], rmeta.at[f], meta_s.at[f], meta_r.at[f], at(1)).wait_recv()
    for m in range(6):
        pos_all[2 * m:2 * m + 2] = rmeta[order[m], 0:2]
        gain_all[2 * m:2 * m + 2] = rmeta[order[m], 2:4]
    positions, gains = pos_all[...], gain_all[...]

    def gain_sum(p):
        return jnp.sum(jnp.where(positions == p, gains, 0.0), axis=0, keepdims=True)

    for j in range(12):
        g_all[j:j + 1] = gain_sum(positions[j:j + 1])
    gain_first, gain_last = gain_sum(0.0), gain_sum(31.0)

    y = lax.broadcasted_iota(jnp.int32, (OWNER_ROWS, 128), 0).astype(F32)
    y16 = lax.broadcasted_iota(jnp.int32, (16, 128), 0).astype(F32)
    top_shift = jnp.where(me == 0, 2.0, 1e6).astype(F32)
    bottom_shift = jnp.where(me == n_tile - 1, -1.0 * OWNER_ROWS - 16.0, 1e6).astype(F32)

    def place(m):
        p0, p1 = pos_all[2 * m:2 * m + 1], pos_all[2 * m + 1:2 * m + 2]
        source_row = jnp.where(lane < 64, p0, p1) * TILE_ROWS + lane_row
        cols = slice(m * 128, (m + 1) * 128)

        def hits(d):
            return jnp.where(jnp.abs(d) == gap, 1.0, 0.0)

        mbuf[:, cols] = hits(y - source_row).astype(BF16)
        mbuf[0:16, cols] = (hits(y16 - source_row) - hits(y16 + source_row + top_shift)).astype(BF16)
        low = OWNER_ROWS - 16.0
        mbuf[OWNER_ROWS - 16:, cols] = (
            hits(y16 + low - source_row) - hits(y16 + source_row + bottom_shift)
        ).astype(BF16)

    def sides(pieces, ends):
        right = [pltpu.roll(x, 1, 1) for x in pieces]
        left = [pltpu.roll(x, 127, 1) for x in pieces]
        zero = jnp.zeros_like(pieces[0])
        before = [zero if ends[0] else right[0]] + right[:-1]
        after = left[1:] + [zero if ends[1] else left[-1]]
        return [
            jnp.where(is_first, a, b) + jnp.where(is_last, d, c)
            for a, b, c, d in zip(before, right, left, after)
        ]

    def spread(b_of, put):
        middle = reps // 2
        for lo, hi, keep in ((0, middle + 1, (0, middle)), (middle - 1, reps, (1, middle + 1))):
            b = [b_of(i) for i in range(lo, hi)]
            ends = (lo == 0, hi == reps)
            kept = slice(*keep)
            two = [(0.5 * Q3) * x for x in b[kept]]
            zero = [(0.5 * Q) * x for x in b[kept]]
            one = [(0.5 * Q2 + 3.0 * Q3) * x for x in b[kept]]
            three = [Q3 * x for x in b[kept]]
            c = sides(b, ends)
            two = [t + (3.0 * Q3) * x for t, x in zip(two, c[kept])]
            zero = [t + (0.5 * Q2) * x for t, x in zip(zero, c[kept])]
            one = [t + Q3 * x for t, x in zip(one, c[kept])]
            c = sides(c, ends)
            zero = [t + (0.5 * Q3) * x + 2.0 * s for t, x, s in zip(zero, c[kept], two)]
            one = [t + (3.0 * Q3) * x for t, x in zip(one, c[kept])]
            c = sides(c, ends)
            zero = [t + Q3 * x for t, x in zip(zero, c[kept])]
            first = (lo + keep[0]) * 128
            for d, v in enumerate((zero, one, two, three)):
                put(d, first, jnp.concatenate(v, axis=1).astype(BF16))

    last_row = jnp.where(up, 31.0, 0.0).astype(F32)
    other_row = jnp.where(up, 0.0, 31.0).astype(F32)

    def work(m):
        e = order[m]
        for k in range(2):
            if m > 0:
                remote(sbuf.at[0, k], rbuf.at[e, k], tile_s.at[0, k], tile_r.at[e, k], at(1)).wait_recv()
            j = 2 * m + k
            p = pos_all[j:j + 1]
            keep_near = jnp.broadcast_to(jnp.where(p == last_row, 1.0, 0.0), (8, 128))
            keep_far = jnp.broadcast_to(jnp.where(p == other_row, 1.0, 0.0), (8, 128))
            scale = ramp * gain_all[j:j + 1]
            share = 1.0 / jnp.maximum(ramp * g_all[j:j + 1], 1.0)

            def unit(ch, carry):
                def weighted(i):
                    lanes = slice(i * 128, i * 128 + 128)
                    w = (rbuf[e, k, ch, :, lanes].astype(F32) - dark_v[ch, :, lanes]) * inv_v[ch, :, lanes] * scale
                    return w.astype(BF16).astype(F32)

                def scaled(i):
                    return weighted(i) * share

                for i in range(reps):
                    w = weighted(i)
                    lanes = slice(i * 128, i * 128 + 128)
                    if m < 4:
                        edge[0, ch, :, lanes] += keep_near * jnp.where(up, w[8:16], w[0:8])
                    if m < 2 or m >= 4:
                        edge[1, ch, :, lanes] += keep_far * jnp.where(up, w[0:8], w[8:16])

                def put(d, first, v):
                    start = m * 128 + k * 64 + d * TILE_ROWS
                    vbuf[ch, start:start + TILE_ROWS, first:first + v.shape[1]] = v

                spread(scaled, put)
                return carry

            lax.fori_loop(0, 2, unit, 0)

    def send_edge(j):
        down = up if j == 0 else jnp.logical_not(up)
        total = jnp.where(down, gain_last, gain_first)
        mark = lax.broadcasted_iota(jnp.int32, (8, width), 0) == 4
        block = [jnp.where(mark, wide(jnp.broadcast_to(total, (8, 128))), edge[j, ch]) for ch in range(2)]
        sblk[j] = jnp.concatenate(block, axis=0).astype(BF16)
        offset = jnp.where(down, 1, -1)
        lands = jnp.where(down, 0, 1)
        send(sblk.at[j], rblk.at[lands], blk_s.at[j], blk_r.at[lands], at(offset))

    for m in range(4):
        work(m)
    send_edge(0)
    for m in range(GROUPS):
        place(m)

    per_channel = width // SPAN

    def chunk(n):
        return n // per_channel, pl.ds(pl.multiple_of(lax.rem(n, per_channel) * SPAN, SPAN), SPAN)

    def nearer(n, carry):
        ch, cols = chunk(n)
        acc[ch, :, cols] = jnp.dot(
            mbuf[:, 0:NEARER], vbuf[ch, 0:NEARER, cols], preferred_element_type=F32
        )
        return carry

    lax.fori_loop(0, 2 * per_channel, nearer, 0)

    for m in range(4, GROUPS):
        work(m)
    send_edge(1)

    def farther(n, carry):
        ch, cols = chunk(n)
        made = acc[ch, :, cols] + jnp.dot(
            mbuf[:, NEARER:], vbuf[ch, NEARER:, cols], preferred_element_type=F32
        )
        out_ref[0, ch, :, cols] = made.astype(BF16)
        rim[ch, 0:16, cols] = made[0:16]
        rim[ch, 16:32, cols] = made[OWNER_ROWS - 16:]
        return carry

    lax.fori_loop(0, 2 * per_channel, farther, 0)

    for j in range(2):
        remote(sstrip.at[j], rstrip.at[j], str_s.at[j], str_r.at[j], at(1)).wait_recv()
        remote(sblk.at[j], rblk.at[j], blk_s.at[j], blk_r.at[j], at(1)).wait_recv()
    shares = []
    for j in range(2):
        inside = jnp.where(me == (0 if j == 0 else n_tile - 1), 0.0, 1.0).astype(F32)
        lo = 8 - 8 * j
        total = rblk[j].astype(F32)[4:5, 0:128]
        shares.append(inside / jnp.maximum(total * ramp[lo:lo + 8], 1.0))

    def beside_rows(ch, carry):
        start = pl.multiple_of(8 * ch, 8)

        def rows(i):
            lanes = slice(i * 128, i * 128 + 128)
            made = []
            for j in range(2):
                got = jnp.where(ch == 0, rblk[j, :, lanes].astype(F32)[0:8], rblk[j, :, lanes].astype(F32)[8:16])
                direct = jnp.where(
                    ch == 0, rstrip[1 - j, :, lanes].astype(F32)[0:8], rstrip[1 - j, :, lanes].astype(F32)[8:16]
                )
                made.append((got + direct + strip[1 + j, ch, :, lanes]) * shares[j])
            return jnp.concatenate([made[1], made[0]], axis=0)

        def put(d, first, v):
            vrim[ch, d * TILE_ROWS:(d + 1) * TILE_ROWS, first:first + v.shape[1]] = v

        spread(rows, put)
        for first in range(0, width, SPAN):
            cols = slice(first, first + SPAN)
            made = rim[ch, :, cols] + jnp.dot(mrim[...], vrim[ch, :, cols], preferred_element_type=F32)
            out_ref[0, ch, 0:16, cols] = made[0:16].astype(BF16)
            out_ref[0, ch, OWNER_ROWS - 16:, cols] = made[16:32].astype(BF16)
        return carry

    lax.fori_loop(0, 2, beside_rows, 0)

    for copy in sends:
        copy.wait_send()

    @pl.when(inner)
    def _():
        for k in range(1, n_plane):
            remote(prof.at[core, plane], prof.at[core, plane], gat_s.at[k], gat_r.at[plane], mate(k)).wait_send()
        to_side.wait_send()


def solution(mesh):
    n_tile, n_plane = mesh.shape["tile"], mesh.shape["plane"]

    def per_device(raw_tiles, flat_profile, dark_profile, destinations, positions, levels):
        width = raw_tiles.shape[-1]
        tile = (2, TILE_ROWS, width)
        dma = pltpu.SemaphoreType.DMA
        return pl.pallas_call(
            functools.partial(stitch_kernel, n_tile, n_plane, width),
            out_shape=pltpu.VMEM((1, 2, OWNER_ROWS, width), BF16),
            in_specs=[pl.BlockSpec(memory_space=pltpu.HBM)] * 6,
            out_specs=pl.BlockSpec(memory_space=pltpu.VMEM),
            scratch_shapes=[
                pltpu.SMEM((1, 8), jnp.int32),
                pltpu.SMEM((1, 8), jnp.int32),
                pltpu.SMEM((1, 8), jnp.int32),
                pltpu.VMEM((8,) + tile, BF16),
                pltpu.VMEM((5, 2) + tile, BF16),
                pltpu.VMEM((6, 2) + tile, BF16),
                pltpu.VMEM((6, 8, 128), F32),
                pltpu.VMEM((6, 8, 128), F32),
                pltpu.VMEM((2, n_plane, 2, TILE_ROWS // n_plane, width), BF16),
                pltpu.VMEM(tile, F32),
                pltpu.VMEM(tile, F32),
                pltpu.VMEM((16, 128), F32),
                pltpu.VMEM((16, 128), F32),
                pltpu.VMEM((16, 128), F32),
                pltpu.VMEM((2, 2, 8, width), F32),
                pltpu.VMEM((4, 2, 8, width), F32),
                pltpu.VMEM((2, 16, width), BF16),
                pltpu.VMEM((2, 16, width), BF16),
                pltpu.VMEM((2, 16, width), BF16),
                pltpu.VMEM((2, 16, width), BF16),
                pltpu.VMEM((2, DEPTH, width), BF16),
                pltpu.VMEM((OWNER_ROWS, DEPTH), BF16),
                pltpu.VMEM((2, OWNER_ROWS, width), F32),
                pltpu.VMEM((2, 32, width), F32),
                pltpu.VMEM((2, 64, width), BF16),
                pltpu.VMEM((32, 64), BF16),
                dma, dma, dma((3,)),
                dma((5, 2)), dma((5, 2)), dma((5,)), dma((5,)),
                dma((n_plane,)), dma((n_plane,)), dma, dma, dma, dma,
                dma((2,)), dma((2,)), dma((2,)), dma((2,)),
            ],
            compiler_params=pltpu.CompilerParams(
                collective_id=0, has_side_effects=True, vmem_limit_bytes=(62 << 20) - (64 << 10)
            ),
            name="stitch",
        )(destinations[:, :, 0], positions, levels, raw_tiles, flat_profile, dark_profile)

    placed = (
        P("plane", "tile", None, None, None),
        P(None, "plane", None),
        P(None, "plane", None),
        P("plane", "tile", None),
        P("plane", "tile"),
        P("plane", "tile"),
    )
    return jax.shard_map(
        per_device, mesh=mesh, in_specs=placed, out_specs=P("plane", None, "tile", None), check_vma=False
    )
```

```python
import functools

import jax
import jax.numpy as jnp
from jax import lax
from jax.experimental import pallas as pl
from jax.experimental.pallas import tpu as pltpu
from jax.sharding import PartitionSpec as P

MESH = pl.DeviceIdType.MESH
F32 = jnp.float32
BF16 = jnp.bfloat16
OWNER_ROWS = 512
TILE_ROWS = 16
NEAR = (-2, -1, 1, 2)
GROUPS = 6
DEPTH = GROUPS * 128
NEARER = 4 * 128
SPAN = 1024
Q = 1.0 / 4.5
Q2 = Q * Q
Q3 = Q2 * Q


def stitch_kernel(
    n_tile, n_plane, width,
    dest_hbm, pos_hbm, level_hbm, raw_ref, flat_ref, dark_ref, out_ref,
    dest_ref, pos_ref, level_ref,
    rawv, sbuf, rbuf, smeta, rmeta, prof, dark_v, inv_v, pos_all, gain_all, g_all,
    edge, strip, sblk, rblk, passing, wbuf, vbuf, mbuf, acc, rim, vrim, mrim,
    raw_sem, own_sem, int_sem, go_sem,
    tile_s, tile_r, meta_s, meta_r, gat_s, gat_r, side_s, side_r, swap_s, swap_r, blk_s, blk_r, pass_s, pass_r,
):
    me = lax.axis_index("tile")
    plane = lax.axis_index("plane")
    core = lax.rem(me, 2)
    column = lax.rem(me // 2, 4)
    up = column >= 2
    inner = jnp.logical_or(column == 1, column == 2)
    half = n_tile // 2
    reps = width // 128

    def at(offset):
        return {"tile": lax.rem(me + offset + n_tile, n_tile), "plane": plane}

    def mate(k):
        return {"tile": me, "plane": lax.rem(plane + k, n_plane)}

    def late_of(device):
        return lax.rem(device // 8, 2)

    is_late = late_of(me)
    late = is_late == 1
    early = is_late == 0
    outer = jnp.logical_not(inner)
    far = jnp.where(up, 3, 0)
    far_offset = jnp.where(up, 2, -2)
    next_far = jnp.where(up, 2, 1)
    next_crosses = core == jnp.where(up, 1, 0)
    crossing = jnp.where(next_crosses, 2, 1)

    def crosses(offset):
        return late_of(lax.rem(me + offset + n_tile, n_tile)) != is_late

    barrier = pltpu.get_barrier_semaphore()
    for offset in NEAR + (half,):
        @pl.when(jnp.logical_or(early, jnp.logical_not(crosses(offset))))
        def _():
            pl.semaphore_signal(barrier, inc=1, device_id=at(offset), device_id_type=MESH)

    @pl.when(inner)
    def _():
        for k in range(1, n_plane):
            pl.semaphore_signal(barrier, inc=1, device_id=mate(k), device_id_type=MESH)

    @pl.when(early)
    def _():
        pl.semaphore_signal(barrier, inc=1, device_id=at(2 * far_offset), device_id_type=MESH)

    loads = [
        pltpu.make_async_copy(src, dst, int_sem.at[j])
        for j, (src, dst) in enumerate(((dest_hbm, dest_ref), (pos_hbm, pos_ref), (level_hbm, level_ref)))
    ]
    for load in loads:
        load.start()
    load_raw = pltpu.make_async_copy(raw_ref.at[0], rawv, raw_sem)
    load_raw.start()

    @pl.when(jnp.logical_and(inner, core == 0))
    def _():
        pltpu.make_async_copy(flat_ref, prof.at[0, plane], own_sem).start()

    @pl.when(jnp.logical_and(inner, core == 1))
    def _():
        pltpu.make_async_copy(dark_ref, prof.at[1, plane], own_sem).start()

    for load in loads:
        load.wait()
    rel = [lax.rem(dest_ref[0, t] - me + 2 + 2 * n_tile, n_tile) for t in range(8)]
    picks = []
    for e, offset in enumerate(NEAR + (half, 0)):
        key = offset + 2
        first, last, hits = jnp.int32(0), jnp.int32(0), jnp.int32(0)
        for t in range(8):
            hit = rel[t] == key
            last = jnp.where(hit, t, last)
            hits = hits + jnp.where(hit, 1, 0)
            first = jnp.where(rel[7 - t] == key, 7 - t, first)
        gain0 = jnp.where(hits > 0, level_ref[0, first], 0).astype(F32)
        gain1 = jnp.where(hits > 1, level_ref[0, last], 0).astype(F32)
        pos0 = pos_ref[0, first].astype(F32)
        pos1 = pos_ref[0, last].astype(F32)
        row = lax.broadcasted_iota(jnp.int32, (8, 128), 0)
        meta = jnp.where(row == 0, pos0, jnp.where(row == 1, pos1, jnp.where(row == 2, gain0, gain1)))
        smeta[e] = meta
        if e == 5:
            rmeta[5] = meta
        picks.append((first, last))
    load_raw.wait()
    for e, (first, last) in enumerate(picks):
        if e == 5:
            rbuf[5, 0] = rawv[first]
            rbuf[5, 1] = rawv[last]
        else:
            sbuf[e, 0] = rawv[first]
            sbuf[e, 1] = rawv[last]

    @pl.when(inner)
    def _():
        pltpu.make_async_copy(flat_ref, prof.at[core, plane], own_sem).wait()

    pl.semaphore_wait(barrier, jnp.where(inner, 4 + n_plane + is_late, jnp.where(late, 6, 5 - crossing)))

    @pl.when(late)
    def _():
        for offset in NEAR:
            @pl.when(crosses(offset))
            def _():
                pl.semaphore_signal(go_sem, inc=1, device_id=at(offset), device_id_type=MESH)

    @pl.when(jnp.logical_and(late, outer))
    def _():
        pl.semaphore_signal(go_sem, inc=1, device_id=at(2 * far_offset), device_id_type=MESH)

    sends = []

    def remote(src, dst, s_sem, r_sem, device):
        return pltpu.make_async_remote_copy(src, dst, s_sem, r_sem, device_id=device, device_id_type=MESH)

    def send(src, dst, s_sem, r_sem, device):
        copy = remote(src, dst, s_sem, r_sem, device)
        copy.start()
        sends.append(copy)

    def slot_at_target(e):
        return 3 - e if e < 4 else 4

    def send_meta(e):
        f = slot_at_target(e)
        return remote(smeta.at[e], rmeta.at[f], meta_s.at[e], meta_r.at[f], at((NEAR + (half,))[e]))

    for e, offset in enumerate(NEAR + (half,)):
        @pl.when(jnp.logical_or(late, jnp.logical_not(crosses(offset))))
        def _():
            send_meta(e).start()

    @pl.when(inner)
    def _():
        for k in range(1, n_plane):
            remote(prof.at[core, plane], prof.at[core, plane], gat_s.at[k], gat_r.at[plane], mate(k)).start()

    def send_tile(e, k, offset):
        return remote(sbuf.at[e, k], rbuf.at[3 - e, k], tile_s.at[e, k], tile_r.at[3 - e, k], at(offset))

    def send_far():
        send_tile(far, 0, far_offset).start()

    def send_next():
        for k in range(2):
            send_tile(next_far, k, jnp.where(up, 1, -1)).start()

    def send_near():
        for j in range(2):
            e = jnp.where(up, j, 3 - j)
            for k in range(2):
                send_tile(e, k, jnp.where(up, j - 2, 2 - j)).start()

    @pl.when(jnp.logical_not(inner))
    def _():
        remote(sbuf.at[far, 1], passing, tile_s.at[far, 1], pass_r, at(-far_offset)).start()

    @pl.when(jnp.logical_and(outer, late))
    def _():
        send_far()

    @pl.when(jnp.logical_and(outer, jnp.logical_or(late, jnp.logical_not(next_crosses))))
    def _():
        send_next()

    for k in range(2):
        send(sbuf.at[4, k], rbuf.at[4, k], tile_s.at[4, k], tile_r.at[4, k], at(half))

    @pl.when(jnp.logical_not(inner))
    def _():
        send_near()

    to_side = remote(prof.at[core], prof.at[core], side_s, side_r, at(far_offset))
    pass_on = remote(passing, rbuf.at[3 - far, 1], pass_s, tile_r.at[3 - far, 1], at(2 * far_offset))
    def forward():
        remote(sbuf.at[far, 1], passing, tile_s.at[far, 1], pass_r, at(-far_offset)).wait_recv()
        pass_on.start()

    @pl.when(jnp.logical_and(inner, late))
    def _():
        forward()

    @pl.when(inner)
    def _():
        for k in range(1, n_plane):
            source = lax.rem(plane + k, n_plane)
            remote(prof.at[core, source], prof.at[core, source], gat_s.at[k], gat_r.at[source], mate(k)).wait_recv()
        to_side.start()
        send_tile(far, 1, far_offset).start()
        send_far()
        send_next()
        send_near()

    @pl.when(jnp.logical_not(inner))
    def _():
        to_side.wait_recv()

    other = {"tile": me + 1 - 2 * core, "plane": plane}
    send(prof.at[core], prof.at[core], swap_s, swap_r, other)

    row16 = lax.broadcasted_iota(jnp.int32, (TILE_ROWS, 128), 0)
    ramp = jnp.minimum(row16 + 1, TILE_ROWS - row16).astype(F32)
    lane = lax.broadcasted_iota(jnp.int32, (1, 128), 1)
    gap = lax.rem(lane // TILE_ROWS, 4).astype(F32)
    lane_row = lax.rem(lane, TILE_ROWS).astype(F32)
    lane16 = lax.broadcasted_iota(jnp.int32, (TILE_ROWS, 128), 1)
    lane_b = lane16.astype(F32).astype(BF16)

    def wide(x):
        return jnp.concatenate([x] * reps, axis=1)

    y32 = lax.broadcasted_iota(jnp.int32, (32, 128), 0)
    y32 = jnp.where(y32 < 16, y32, y32 + OWNER_ROWS - 32).astype(F32)
    rim_row = lax.rem(lane, 8).astype(F32)
    rim_row = jnp.where(rim_row < 4, rim_row + OWNER_ROWS, rim_row - 8.0)
    rim_hit = jnp.where(jnp.abs(y32 - rim_row) == gap, 1.0, 0.0)
    for ch in range(2):
        own = lax.rem(lane // 8, 2) == ch
        mrim[ch] = jnp.where(own, rim_hit, 0.0).astype(BF16)[:, 0:64]
    edge[...] = jnp.zeros(edge.shape, F32)
    pos_all[...] = jnp.full((16, 128), -99.0, F32)
    gain_all[...] = jnp.zeros((16, 128), F32)

    remote(prof.at[1 - core], prof.at[1 - core], swap_s, swap_r, other).wait_recv()
    part = TILE_ROWS // n_plane
    for p in range(n_plane):
        inv_v[:, p * part:(p + 1) * part, :] = 1.0 / prof[0, p].astype(F32)
        dark_v[:, p * part:(p + 1) * part, :] = prof[1, p].astype(F32)

    row_wide = lax.broadcasted_iota(jnp.int32, (TILE_ROWS, width), 0)
    gain_row = jnp.logical_or(row_wide == 3, row_wide == 12)
    gain_row16 = jnp.logical_or(row16 == 3, row16 == 12)

    for e in range(4):
        lo, at_pos = (8, 31.0) if e < 2 else (0, 0.0)
        for ch in range(2):
            total = None
            for k in range(2):
                keep = jnp.where(smeta[e, k:k + 1, :] == at_pos, 1.0, 0.0)
                scale = wide(ramp[lo:lo + 8] * smeta[e, 2 + k:3 + k, :])
                tile = sbuf[e, k, ch].astype(F32)[lo:lo + 8]
                w = (tile - dark_v[ch, lo:lo + 8]) * inv_v[ch, lo:lo + 8] * scale
                w = jnp.where(gain_row[lo:lo + 8], wide(smeta[e, 2 + k:3 + k, :]), w.astype(BF16).astype(F32))
                w = w * wide(jnp.broadcast_to(keep, (8, 128)))
                total = w if total is None else total + w
            strip[e, ch] = total
    order = (5, 4) + tuple(jnp.where(up, a, 3 - a) for a in (1, 0, 2, 3))

    def take_meta(m):
        if m > 0:
            f = order[m]
            remote(smeta.at[0], rmeta.at[f], meta_s.at[0], meta_r.at[f], at(1)).wait_recv()
        pos_all[2 * m:2 * m + 2] = rmeta[order[m], 0:2]
        gain_all[2 * m:2 * m + 2] = rmeta[order[m], 2:4]

    for m in range(4):
        take_meta(m)

    y = lax.broadcasted_iota(jnp.int32, (OWNER_ROWS, 128), 0).astype(F32)
    y16 = lax.broadcasted_iota(jnp.int32, (16, 128), 0).astype(F32)
    top_shift = jnp.where(me == 0, 2.0, 1e6).astype(F32)
    bottom_shift = jnp.where(me == n_tile - 1, -1.0 * OWNER_ROWS - 16.0, 1e6).astype(F32)

    def place(m):
        p0, p1 = pos_all[2 * m:2 * m + 1], pos_all[2 * m + 1:2 * m + 2]
        source_row = jnp.where(lane < 64, p0, p1) * TILE_ROWS + lane_row
        cols = slice(m * 128, (m + 1) * 128)

        def hits(d):
            return jnp.where(jnp.abs(d) == gap, 1.0, 0.0)

        mbuf[:, cols] = hits(y - source_row).astype(BF16)
        mbuf[0:16, cols] = (hits(y16 - source_row) - hits(y16 + source_row + top_shift)).astype(BF16)
        low = OWNER_ROWS - 16.0
        mbuf[OWNER_ROWS - 16:, cols] = (
            hits(y16 + low - source_row) - hits(y16 + source_row + bottom_shift)
        ).astype(BF16)

    def spread(pieces, share, put):
        nothing = jnp.zeros((TILE_ROWS, 128), BF16)
        right, left = {}, {}
        for d in (1, 2, 3):
            right[d] = [pltpu.roll(x, d, 1) for x in pieces]
            left[d] = [pltpu.roll(x, 128 - d, 1) for x in pieces]
        for i in range(reps):
            x = pieces[i].astype(F32)
            s = {}
            for d in (1, 2, 3):
                r = jnp.where(lane_b < d, right[d][i - 1] if i else nothing, right[d][i]).astype(F32)
                l = jnp.where(lane_b >= 128 - d, left[d][i + 1] if i + 1 < reps else nothing, left[d][i]).astype(F32)
                s[d] = r + l
                if d == 1:
                    r1, l1 = r, l
            second, third = s[2], s[3]
            if i == 0:
                second = second - jnp.where(lane16 == 0, x, 0.0)
                third = third - jnp.where(lane16 == 0, l1, jnp.where(lane16 == 1, r1, 0.0))
            if i == reps - 1:
                second = second - jnp.where(lane16 == 127, x, 0.0)
                third = third - jnp.where(lane16 == 127, r1, jnp.where(lane16 == 126, l1, 0.0))
            zero = (0.5 * Q + 2.0 * Q3) * x + (0.5 * Q2 + 9.0 * Q3) * s[1] + (0.5 * Q3) * second + Q3 * third
            one = (0.5 * Q2 + 9.0 * Q3) * x + Q3 * s[1] + (3.0 * Q3) * second
            two = (0.5 * Q3) * x + (3.0 * Q3) * s[1]
            for d, v in enumerate((zero, one, two, Q3 * x)):
                put(d, slice(i * 128, i * 128 + 128), (v * share).astype(BF16))

    last_row = jnp.where(up, 31.0, 0.0).astype(F32)
    other_row = jnp.where(up, 0.0, 31.0).astype(F32)

    def weigh(m, k):
        e = order[m]
        if m > 0:
            remote(sbuf.at[0, k], rbuf.at[e, k], tile_s.at[0, k], tile_r.at[e, k], at(1)).wait_recv()
        j = 2 * m + k
        p = pos_all[j:j + 1]
        keep_near = jnp.broadcast_to(jnp.where(p == last_row, 1.0, 0.0), (8, 128))
        keep_far = jnp.broadcast_to(jnp.where(p == other_row, 1.0, 0.0), (8, 128))
        scale = ramp * gain_all[j:j + 1]

        def unit(ch, carry):
            for i in range(reps):
                lanes = slice(i * 128, i * 128 + 128)
                w = (rbuf[e, k, ch, :, lanes].astype(F32) - dark_v[ch, :, lanes]) * inv_v[ch, :, lanes] * scale
                w = w.astype(BF16)
                wbuf[j, ch, :, lanes] = w
                w = jnp.where(gain_row16, gain_all[j:j + 1], w.astype(F32))
                if m < 4:
                    edge[0, ch, :, lanes] += keep_near * jnp.where(up, w[8:16], w[0:8])
                if m < 2 or m >= 4:
                    edge[1, ch, :, lanes] += keep_far * jnp.where(up, w[0:8], w[8:16])
            return carry

        lax.fori_loop(0, 2, unit, 0)

    def filter_columns(m, k):
        j = 2 * m + k
        share = 1.0 / jnp.maximum(ramp * g_all[j:j + 1], 1.0)

        def unit(ch, carry):
            def put(d, lanes, v):
                start = m * 128 + k * 64 + d * TILE_ROWS
                vbuf[ch, start:start + TILE_ROWS, lanes] = v

            spread([wbuf[j, ch, :, i * 128:i * 128 + 128] for i in range(reps)], share, put)
            return carry

        lax.fori_loop(0, 2, unit, 0)

    def send_edge(j):
        down = up if j == 0 else jnp.logical_not(up)
        row8 = lax.broadcasted_iota(jnp.int32, (8, width), 0)
        block = []
        for ch in range(2):
            sums, ours = edge[j, ch], jnp.where(down, strip[3, ch], strip[0, ch])
            below = jnp.where(down, ours, sums)
            above = jnp.where(down, sums, ours)
            block.append(jnp.where(row8 < 4, below, above))
        sblk[j] = jnp.concatenate(block, axis=0).astype(BF16)
        offset = jnp.where(down, 1, -1)
        lands = jnp.where(down, 0, 1)
        send(sblk.at[j], rblk.at[lands], blk_s.at[j], blk_r.at[lands], at(offset))

    for m in range(4):
        for k in range(2):
            weigh(m, k)

    @pl.when(jnp.logical_and(early, outer))
    def _():
        pl.semaphore_wait(go_sem, crossing)
        for e, offset in enumerate(NEAR):
            @pl.when(crosses(offset))
            def _():
                send_meta(e).start()
        send_far()

        @pl.when(next_crosses)
        def _():
            send_next()

    @pl.when(jnp.logical_and(early, inner))
    def _():
        pl.semaphore_wait(go_sem, 1)
        forward()

    send_edge(0)
    for m in range(4, GROUPS):
        take_meta(m)
    positions, gains = pos_all[...], gain_all[...]
    for j in range(12):
        own = jnp.where(positions == positions[j:j + 1], gains, 0.0)
        g_all[j:j + 1] = jnp.sum(own, axis=0, keepdims=True)
    for m in range(GROUPS):
        place(m)
    for m in range(4):
        for k in range(2):
            filter_columns(m, k)

    per_channel = width // SPAN

    def chunk(n):
        return n // per_channel, pl.ds(pl.multiple_of(lax.rem(n, per_channel) * SPAN, SPAN), SPAN)

    def nearer(n, carry):
        ch, cols = chunk(n)
        acc[ch, :, cols] = jnp.dot(
            mbuf[:, 0:NEARER], vbuf[ch, 0:NEARER, cols], preferred_element_type=F32
        )
        return carry

    lax.fori_loop(0, 2 * per_channel, nearer, 0)

    for k in range(2):
        for m in range(4, GROUPS):
            weigh(m, k)
        if k == 1:
            send_edge(1)
        for m in range(4, GROUPS):
            filter_columns(m, k)

    def farther(n, carry):
        ch, cols = chunk(n)
        made = acc[ch, :, cols] + jnp.dot(
            mbuf[:, NEARER:], vbuf[ch, NEARER:, cols], preferred_element_type=F32
        )
        out_ref[0, ch, :, cols] = made.astype(BF16)
        rim[ch, 0:16, cols] = made[0:16]
        rim[ch, 16:32, cols] = made[OWNER_ROWS - 16:]
        return carry

    lax.fori_loop(0, 2 * per_channel, farther, 0)

    for j in range(2):
        remote(sblk.at[j], rblk.at[j], blk_s.at[j], blk_r.at[j], at(1)).wait_recv()
    row_in = lax.rem(row16, 8)
    ramp_rim = jnp.minimum(row_in + 1, 8 - row_in).astype(F32)
    inside = jnp.where(
        row_in < 4, jnp.where(me == n_tile - 1, 0.0, 1.0).astype(F32), jnp.where(me == 0, 0.0, 1.0).astype(F32)
    )
    inside = jnp.where(jnp.logical_or(row_in == 3, row_in == 4), 0.0, inside)
    beside_rows = []
    for i in range(reps):
        lanes = slice(i * 128, i * 128 + 128)
        below = jnp.concatenate([strip[2, 0, :, lanes], strip[2, 1, :, lanes]], axis=0)
        above = jnp.concatenate([strip[1, 0, :, lanes], strip[1, 1, :, lanes]], axis=0)
        rows = rblk[0, :, lanes].astype(F32) + rblk[1, :, lanes].astype(F32) + jnp.where(row_in < 4, below, above)
        if i == 0:
            weights = jnp.where(row_in < 4, rows[3:4], rows[4:5]) * ramp_rim
        beside_rows.append(rows.astype(BF16))
    rim_share = inside / jnp.maximum(weights, 1.0)

    def put_rim(d, lanes, v):
        vrim[d * TILE_ROWS:(d + 1) * TILE_ROWS, lanes] = v

    spread(beside_rows, rim_share, put_rim)
    for ch in range(2):
        for first in range(0, width, SPAN):
            cols = slice(first, first + SPAN)
            made = rim[ch, :, cols] + jnp.dot(mrim[ch], vrim[:, cols], preferred_element_type=F32)
            out_ref[0, ch, 0:16, cols] = made[0:16].astype(BF16)
            out_ref[0, ch, OWNER_ROWS - 16:, cols] = made[16:32].astype(BF16)

    for e in range(4):
        for k in range(2):
            send_tile(e, k, NEAR[e]).wait_send()
    for e in range(5):
        send_meta(e).wait_send()
    for copy in sends:
        copy.wait_send()

    @pl.when(inner)
    def _():
        for k in range(1, n_plane):
            remote(prof.at[core, plane], prof.at[core, plane], gat_s.at[k], gat_r.at[plane], mate(k)).wait_send()
        to_side.wait_send()
        pass_on.wait_send()


def solution(mesh):
    n_tile, n_plane = mesh.shape["tile"], mesh.shape["plane"]

    def per_device(raw_tiles, flat_profile, dark_profile, destinations, positions, levels):
        width = raw_tiles.shape[-1]
        tile = (2, TILE_ROWS, width)
        dma = pltpu.SemaphoreType.DMA
        return pl.pallas_call(
            functools.partial(stitch_kernel, n_tile, n_plane, width),
            out_shape=pltpu.VMEM((1, 2, OWNER_ROWS, width), BF16),
            in_specs=[pl.BlockSpec(memory_space=pltpu.HBM)] * 6,
            out_specs=pl.BlockSpec(memory_space=pltpu.VMEM),
            scratch_shapes=[
                pltpu.SMEM((1, 8), jnp.int32),
                pltpu.SMEM((1, 8), jnp.int32),
                pltpu.SMEM((1, 8), jnp.int32),
                pltpu.VMEM((8,) + tile, BF16),
                pltpu.VMEM((5, 2) + tile, BF16),
                pltpu.VMEM((6, 2) + tile, BF16),
                pltpu.VMEM((6, 8, 128), F32),
                pltpu.VMEM((6, 8, 128), F32),
                pltpu.VMEM((2, n_plane, 2, TILE_ROWS // n_plane, width), BF16),
                pltpu.VMEM(tile, F32),
                pltpu.VMEM(tile, F32),
                pltpu.VMEM((16, 128), F32),
                pltpu.VMEM((16, 128), F32),
                pltpu.VMEM((16, 128), F32),
                pltpu.VMEM((2, 2, 8, width), F32),
                pltpu.VMEM((4, 2, 8, width), F32),
                pltpu.VMEM((2, 16, width), BF16),
                pltpu.VMEM((2, 16, width), BF16),
                pltpu.VMEM(tile, BF16),
                pltpu.VMEM((12,) + tile, BF16),
                pltpu.VMEM((2, DEPTH, width), BF16),
                pltpu.VMEM((OWNER_ROWS, DEPTH), BF16),
                pltpu.VMEM((2, OWNER_ROWS, width), F32),
                pltpu.VMEM((2, 32, width), F32),
                pltpu.VMEM((64, width), BF16),
                pltpu.VMEM((2, 32, 64), BF16),
                dma, dma, dma((3,)), pltpu.SemaphoreType.REGULAR,
                dma((5, 2)), dma((5, 2)), dma((5,)), dma((5,)),
                dma((n_plane,)), dma((n_plane,)), dma, dma, dma, dma,
                dma((2,)), dma((2,)), dma, dma,
            ],
            compiler_params=pltpu.CompilerParams(
                collective_id=0, has_side_effects=True, vmem_limit_bytes=(62 << 20) - (64 << 10)
            ),
            name="stitch",
        )(destinations[:, :, 0], positions, levels, raw_tiles, flat_profile, dark_profile)

    placed = (
        P("plane", "tile", None, None, None),
        P(None, "plane", None),
        P(None, "plane", None),
        P("plane", "tile", None),
        P("plane", "tile"),
        P("plane", "tile"),
    )
    return jax.shard_map(
        per_device, mesh=mesh, in_specs=placed, out_specs=P("plane", None, "tile", None), check_vma=False
    )
```

```python
import functools

import jax
import jax.numpy as jnp
from jax import lax
from jax.experimental import pallas as pl
from jax.experimental.pallas import tpu as pltpu
from jax.sharding import PartitionSpec as P

MESH = pl.DeviceIdType.MESH
F32 = jnp.float32
BF16 = jnp.bfloat16
OWNER_ROWS = 512
TILE_ROWS = 16
NEAR = (-2, -1, 1, 2)
GROUPS = 6
DEPTH = GROUPS * 128
NEARER = 4 * 128
SPAN = 1024
Q = 1.0 / 4.5
Q2 = Q * Q
Q3 = Q2 * Q


def stitch_kernel(
    n_tile, n_plane, width,
    dest_hbm, pos_hbm, level_hbm, raw_ref, flat_ref, dark_ref, out_ref,
    dest_ref, pos_ref, level_ref,
    rawv, sbuf, rbuf, smeta, rmeta, prof, dark_v, inv_v, pos_all, gain_all, g_all,
    edge, strip, sblk, rblk, passing, wbuf, vbuf, mbuf, acc, rim, vrim, mrim,
    raw_sem, own_sem, int_sem, go_sem,
    tile_s, tile_r, meta_s, meta_r, gat_s, gat_r, side_s, side_r, swap_s, swap_r, blk_s, blk_r, pass_s, pass_r,
):
    me = lax.axis_index("tile")
    plane = lax.axis_index("plane")
    core = lax.rem(me, 2)
    column = lax.rem(me // 2, 4)
    up = column >= 2
    inner = jnp.logical_or(column == 1, column == 2)
    half = n_tile // 2
    reps = width // 128

    def at(offset):
        return {"tile": lax.rem(me + offset + n_tile, n_tile), "plane": plane}

    def mate(k):
        return {"tile": me, "plane": lax.rem(plane + k, n_plane)}

    def late_of(device):
        return lax.rem(device // 8, 2)

    is_late = late_of(me)
    late = is_late == 1
    early = is_late == 0
    outer = jnp.logical_not(inner)
    far = jnp.where(up, 3, 0)
    far_offset = jnp.where(up, 2, -2)
    next_far = jnp.where(up, 2, 1)
    next_crosses = core == jnp.where(up, 1, 0)
    crossing = jnp.where(next_crosses, 2, 1)

    def crosses(offset):
        return late_of(lax.rem(me + offset + n_tile, n_tile)) != is_late

    barrier = pltpu.get_barrier_semaphore()
    for offset in NEAR + (half,):
        @pl.when(jnp.logical_or(early, jnp.logical_not(crosses(offset))))
        def _():
            pl.semaphore_signal(barrier, inc=1, device_id=at(offset), device_id_type=MESH)

    @pl.when(inner)
    def _():
        for k in range(1, n_plane):
            pl.semaphore_signal(barrier, inc=1, device_id=mate(k), device_id_type=MESH)

    @pl.when(early)
    def _():
        pl.semaphore_signal(barrier, inc=1, device_id=at(2 * far_offset), device_id_type=MESH)

    loads = [
        pltpu.make_async_copy(src, dst, int_sem.at[j])
        for j, (src, dst) in enumerate(((dest_hbm, dest_ref), (pos_hbm, pos_ref), (level_hbm, level_ref)))
    ]
    for load in loads:
        load.start()
    load_raw = pltpu.make_async_copy(raw_ref.at[0], rawv, raw_sem)
    load_raw.start()

    @pl.when(jnp.logical_and(inner, core == 0))
    def _():
        pltpu.make_async_copy(flat_ref, prof.at[0, plane], own_sem).start()

    @pl.when(jnp.logical_and(inner, core == 1))
    def _():
        pltpu.make_async_copy(dark_ref, prof.at[1, plane], own_sem).start()

    for load in loads:
        load.wait()
    rel = [lax.rem(dest_ref[0, t] - me + 2 + 2 * n_tile, n_tile) for t in range(8)]
    picks = []
    for e, offset in enumerate(NEAR + (half, 0)):
        key = offset + 2
        first, last, hits = jnp.int32(0), jnp.int32(0), jnp.int32(0)
        for t in range(8):
            hit = rel[t] == key
            last = jnp.where(hit, t, last)
            hits = hits + jnp.where(hit, 1, 0)
            first = jnp.where(rel[7 - t] == key, 7 - t, first)
        gain0 = jnp.where(hits > 0, level_ref[0, first], 0).astype(F32)
        gain1 = jnp.where(hits > 1, level_ref[0, last], 0).astype(F32)
        pos0 = pos_ref[0, first].astype(F32)
        pos1 = pos_ref[0, last].astype(F32)
        row = lax.broadcasted_iota(jnp.int32, (8, 128), 0)
        meta = jnp.where(row == 0, pos0, jnp.where(row == 1, pos1, jnp.where(row == 2, gain0, gain1)))
        smeta[e] = meta
        if e == 5:
            rmeta[5] = meta
        picks.append((first, last))
    load_raw.wait()
    for e, (first, last) in enumerate(picks):
        if e == 5:
            rbuf[5, 0] = rawv[first]
            rbuf[5, 1] = rawv[last]
        else:
            sbuf[e, 0] = rawv[first]
            sbuf[e, 1] = rawv[last]

    @pl.when(inner)
    def _():
        pltpu.make_async_copy(flat_ref, prof.at[core, plane], own_sem).wait()

    pl.semaphore_wait(barrier, jnp.where(inner, 4 + n_plane + is_late, jnp.where(late, 6, 5 - crossing)))

    @pl.when(late)
    def _():
        for offset in NEAR:
            @pl.when(crosses(offset))
            def _():
                pl.semaphore_signal(go_sem, inc=1, device_id=at(offset), device_id_type=MESH)

    @pl.when(jnp.logical_and(late, outer))
    def _():
        pl.semaphore_signal(go_sem, inc=1, device_id=at(2 * far_offset), device_id_type=MESH)

    sends = []

    def remote(src, dst, s_sem, r_sem, device):
        return pltpu.make_async_remote_copy(src, dst, s_sem, r_sem, device_id=device, device_id_type=MESH)

    def send(src, dst, s_sem, r_sem, device):
        copy = remote(src, dst, s_sem, r_sem, device)
        copy.start()
        sends.append(copy)

    def slot_at_target(e):
        return 3 - e if e < 4 else 4

    def send_meta(e):
        f = slot_at_target(e)
        return remote(smeta.at[e], rmeta.at[f], meta_s.at[e], meta_r.at[f], at((NEAR + (half,))[e]))

    for e, offset in enumerate(NEAR + (half,)):
        @pl.when(jnp.logical_or(late, jnp.logical_not(crosses(offset))))
        def _():
            send_meta(e).start()

    @pl.when(inner)
    def _():
        for k in range(1, n_plane):
            remote(prof.at[core, plane], prof.at[core, plane], gat_s.at[k], gat_r.at[plane], mate(k)).start()

    def send_tile(e, k, offset):
        return remote(sbuf.at[e, k], rbuf.at[3 - e, k], tile_s.at[e, k], tile_r.at[3 - e, k], at(offset))

    def send_far():
        send_tile(far, 0, far_offset).start()

    def send_next():
        for k in range(2):
            send_tile(next_far, k, jnp.where(up, 1, -1)).start()

    def send_near():
        for j in range(2):
            e = jnp.where(up, j, 3 - j)
            for k in range(2):
                send_tile(e, k, jnp.where(up, j - 2, 2 - j)).start()

    @pl.when(jnp.logical_not(inner))
    def _():
        remote(sbuf.at[far, 1], passing, tile_s.at[far, 1], pass_r, at(-far_offset)).start()

    @pl.when(jnp.logical_and(outer, late))
    def _():
        send_far()

    @pl.when(jnp.logical_and(outer, jnp.logical_or(late, jnp.logical_not(next_crosses))))
    def _():
        send_next()

    for k in range(2):
        send(sbuf.at[4, k], rbuf.at[4, k], tile_s.at[4, k], tile_r.at[4, k], at(half))

    @pl.when(jnp.logical_not(inner))
    def _():
        send_near()

    to_side = remote(prof.at[core], prof.at[core], side_s, side_r, at(far_offset))
    pass_on = remote(passing, rbuf.at[3 - far, 1], pass_s, tile_r.at[3 - far, 1], at(2 * far_offset))
    def forward():
        remote(sbuf.at[far, 1], passing, tile_s.at[far, 1], pass_r, at(-far_offset)).wait_recv()
        pass_on.start()

    @pl.when(jnp.logical_and(inner, late))
    def _():
        forward()

    @pl.when(inner)
    def _():
        for k in range(1, n_plane):
            source = lax.rem(plane + k, n_plane)
            remote(prof.at[core, source], prof.at[core, source], gat_s.at[k], gat_r.at[source], mate(k)).wait_recv()
        to_side.start()
        send_tile(far, 1, far_offset).start()
        send_far()
        send_next()
        send_near()

    @pl.when(jnp.logical_and(early, outer))
    def _():
        pl.semaphore_wait(go_sem, crossing)
        for e, offset in enumerate(NEAR):
            @pl.when(crosses(offset))
            def _():
                send_meta(e).start()
        send_far()

        @pl.when(next_crosses)
        def _():
            send_next()

    @pl.when(jnp.logical_and(early, inner))
    def _():
        pl.semaphore_wait(go_sem, 1)
        forward()

    @pl.when(jnp.logical_not(inner))
    def _():
        to_side.wait_recv()

    other = {"tile": me + 1 - 2 * core, "plane": plane}
    send(prof.at[core], prof.at[core], swap_s, swap_r, other)

    row16 = lax.broadcasted_iota(jnp.int32, (TILE_ROWS, 128), 0)
    ramp = jnp.minimum(row16 + 1, TILE_ROWS - row16).astype(F32)
    lane = lax.broadcasted_iota(jnp.int32, (1, 128), 1)
    gap = lax.rem(lane // TILE_ROWS, 4).astype(F32)
    lane_row = lax.rem(lane, TILE_ROWS).astype(F32)
    lane16 = lax.broadcasted_iota(jnp.int32, (TILE_ROWS, 128), 1)
    lane_b = lane16.astype(F32).astype(BF16)

    def wide(x):
        return jnp.concatenate([x] * reps, axis=1)

    y32 = lax.broadcasted_iota(jnp.int32, (32, 128), 0)
    y32 = jnp.where(y32 < 16, y32, y32 + OWNER_ROWS - 32).astype(F32)
    rim_row = lax.rem(lane, 8).astype(F32)
    rim_row = jnp.where(rim_row < 4, rim_row + OWNER_ROWS, rim_row - 8.0)
    rim_hit = jnp.where(jnp.abs(y32 - rim_row) == gap, 1.0, 0.0)
    for ch in range(2):
        own = lax.rem(lane // 8, 2) == ch
        mrim[ch] = jnp.where(own, rim_hit, 0.0).astype(BF16)[:, 0:64]
    edge[...] = jnp.zeros(edge.shape, F32)
    pos_all[...] = jnp.full((16, 128), -99.0, F32)
    gain_all[...] = jnp.zeros((16, 128), F32)

    remote(prof.at[1 - core], prof.at[1 - core], swap_s, swap_r, other).wait_recv()
    part = TILE_ROWS // n_plane
    for p in range(n_plane):
        inv_v[:, p * part:(p + 1) * part, :] = 1.0 / prof[0, p].astype(F32)
        dark_v[:, p * part:(p + 1) * part, :] = prof[1, p].astype(F32)

    row_wide = lax.broadcasted_iota(jnp.int32, (TILE_ROWS, width), 0)
    gain_row = jnp.logical_or(row_wide == 3, row_wide == 12)
    gain_row16 = jnp.logical_or(row16 == 3, row16 == 12)

    for e in range(4):
        lo, at_pos = (8, 31.0) if e < 2 else (0, 0.0)
        for ch in range(2):
            total = None
            for k in range(2):
                keep = jnp.where(smeta[e, k:k + 1, :] == at_pos, 1.0, 0.0)
                scale = wide(ramp[lo:lo + 8] * smeta[e, 2 + k:3 + k, :])
                tile = sbuf[e, k, ch].astype(F32)[lo:lo + 8]
                w = (tile - dark_v[ch, lo:lo + 8]) * inv_v[ch, lo:lo + 8] * scale
                w = jnp.where(gain_row[lo:lo + 8], wide(smeta[e, 2 + k:3 + k, :]), w.astype(BF16).astype(F32))
                w = w * wide(jnp.broadcast_to(keep, (8, 128)))
                total = w if total is None else total + w
            strip[e, ch] = total
    order = (5, 4) + tuple(jnp.where(up, a, 3 - a) for a in (1, 0, 2, 3))

    def take_meta(m):
        if m > 0:
            f = order[m]
            remote(smeta.at[0], rmeta.at[f], meta_s.at[0], meta_r.at[f], at(1)).wait_recv()
        pos_all[2 * m:2 * m + 2] = rmeta[order[m], 0:2]
        gain_all[2 * m:2 * m + 2] = rmeta[order[m], 2:4]

    for m in range(4):
        take_meta(m)

    y = lax.broadcasted_iota(jnp.int32, (OWNER_ROWS, 128), 0).astype(F32)
    y16 = lax.broadcasted_iota(jnp.int32, (16, 128), 0).astype(F32)
    top_shift = jnp.where(me == 0, 2.0, 1e6).astype(F32)
    bottom_shift = jnp.where(me == n_tile - 1, -1.0 * OWNER_ROWS - 16.0, 1e6).astype(F32)

    def place(m):
        p0, p1 = pos_all[2 * m:2 * m + 1], pos_all[2 * m + 1:2 * m + 2]
        source_row = jnp.where(lane < 64, p0, p1) * TILE_ROWS + lane_row
        cols = slice(m * 128, (m + 1) * 128)

        def hits(d):
            return jnp.where(jnp.abs(d) == gap, 1.0, 0.0)

        mbuf[:, cols] = hits(y - source_row).astype(BF16)
        mbuf[0:16, cols] = (hits(y16 - source_row) - hits(y16 + source_row + top_shift)).astype(BF16)
        low = OWNER_ROWS - 16.0
        mbuf[OWNER_ROWS - 16:, cols] = (
            hits(y16 + low - source_row) - hits(y16 + source_row + bottom_shift)
        ).astype(BF16)

    def spread(pieces, share, put):
        nothing = jnp.zeros((TILE_ROWS, 128), BF16)
        right, left = {}, {}
        for d in (1, 2, 3):
            right[d] = [pltpu.roll(x, d, 1) for x in pieces]
            left[d] = [pltpu.roll(x, 128 - d, 1) for x in pieces]
        for i in range(reps):
            x = pieces[i].astype(F32)
            s = {}
            for d in (1, 2, 3):
                r = jnp.where(lane_b < d, right[d][i - 1] if i else nothing, right[d][i]).astype(F32)
                l = jnp.where(lane_b >= 128 - d, left[d][i + 1] if i + 1 < reps else nothing, left[d][i]).astype(F32)
                s[d] = r + l
                if d == 1:
                    r1, l1 = r, l
            second, third = s[2], s[3]
            if i == 0:
                second = second - jnp.where(lane16 == 0, x, 0.0)
                third = third - jnp.where(lane16 == 0, l1, jnp.where(lane16 == 1, r1, 0.0))
            if i == reps - 1:
                second = second - jnp.where(lane16 == 127, x, 0.0)
                third = third - jnp.where(lane16 == 127, r1, jnp.where(lane16 == 126, l1, 0.0))
            zero = (0.5 * Q + 2.0 * Q3) * x + (0.5 * Q2 + 9.0 * Q3) * s[1] + (0.5 * Q3) * second + Q3 * third
            one = (0.5 * Q2 + 9.0 * Q3) * x + Q3 * s[1] + (3.0 * Q3) * second
            two = (0.5 * Q3) * x + (3.0 * Q3) * s[1]
            for d, v in enumerate((zero, one, two, Q3 * x)):
                put(d, slice(i * 128, i * 128 + 128), (v * share).astype(BF16))

    last_row = jnp.where(up, 31.0, 0.0).astype(F32)
    other_row = jnp.where(up, 0.0, 31.0).astype(F32)

    def weigh(m, k):
        e = order[m]
        if m > 0:
            remote(sbuf.at[0, k], rbuf.at[e, k], tile_s.at[0, k], tile_r.at[e, k], at(1)).wait_recv()
        j = 2 * m + k
        p = pos_all[j:j + 1]
        keep_near = jnp.broadcast_to(jnp.where(p == last_row, 1.0, 0.0), (8, 128))
        keep_far = jnp.broadcast_to(jnp.where(p == other_row, 1.0, 0.0), (8, 128))
        scale = ramp * gain_all[j:j + 1]

        def unit(ch, carry):
            for i in range(reps):
                lanes = slice(i * 128, i * 128 + 128)
                w = (rbuf[e, k, ch, :, lanes].astype(F32) - dark_v[ch, :, lanes]) * inv_v[ch, :, lanes] * scale
                w = w.astype(BF16)
                wbuf[j, ch, :, lanes] = w
                w = jnp.where(gain_row16, gain_all[j:j + 1], w.astype(F32))
                if m < 4:
                    edge[0, ch, :, lanes] += keep_near * jnp.where(up, w[8:16], w[0:8])
                if m < 2 or m >= 4:
                    edge[1, ch, :, lanes] += keep_far * jnp.where(up, w[0:8], w[8:16])
            return carry

        lax.fori_loop(0, 2, unit, 0)

    def filter_columns(m, k):
        j = 2 * m + k
        share = 1.0 / jnp.maximum(ramp * g_all[j:j + 1], 1.0)

        def unit(ch, carry):
            def put(d, lanes, v):
                start = m * 128 + k * 64 + d * TILE_ROWS
                vbuf[ch, start:start + TILE_ROWS, lanes] = v

            spread([wbuf[j, ch, :, i * 128:i * 128 + 128] for i in range(reps)], share, put)
            return carry

        lax.fori_loop(0, 2, unit, 0)

    def send_edge(j):
        down = up if j == 0 else jnp.logical_not(up)
        row8 = lax.broadcasted_iota(jnp.int32, (8, width), 0)
        block = []
        for ch in range(2):
            sums, ours = edge[j, ch], jnp.where(down, strip[3, ch], strip[0, ch])
            below = jnp.where(down, ours, sums)
            above = jnp.where(down, sums, ours)
            block.append(jnp.where(row8 < 4, below, above))
        sblk[j] = jnp.concatenate(block, axis=0).astype(BF16)
        offset = jnp.where(down, 1, -1)
        lands = jnp.where(down, 0, 1)
        send(sblk.at[j], rblk.at[lands], blk_s.at[j], blk_r.at[lands], at(offset))

    for m in range(4):
        for k in range(2):
            weigh(m, k)

    send_edge(0)
    for m in range(4, GROUPS):
        take_meta(m)
    positions, gains = pos_all[...], gain_all[...]
    for j in range(12):
        own = jnp.where(positions == positions[j:j + 1], gains, 0.0)
        g_all[j:j + 1] = jnp.sum(own, axis=0, keepdims=True)
    for m in range(GROUPS):
        place(m)
    for m in range(4):
        for k in range(2):
            filter_columns(m, k)

    per_channel = width // SPAN

    def chunk(n):
        return n // per_channel, pl.ds(pl.multiple_of(lax.rem(n, per_channel) * SPAN, SPAN), SPAN)

    def nearer(n, carry):
        ch, cols = chunk(n)
        acc[ch, :, cols] = jnp.dot(
            mbuf[:, 0:NEARER], vbuf[ch, 0:NEARER, cols], preferred_element_type=F32
        )
        return carry

    lax.fori_loop(0, 2 * per_channel, nearer, 0)

    for k in range(2):
        for m in range(4, GROUPS):
            weigh(m, k)
        if k == 1:
            send_edge(1)
        for m in range(4, GROUPS):
            filter_columns(m, k)

    def farther(n, carry):
        ch, cols = chunk(n)
        made = acc[ch, :, cols] + jnp.dot(
            mbuf[:, NEARER:], vbuf[ch, NEARER:, cols], preferred_element_type=F32
        )
        out_ref[0, ch, :, cols] = made.astype(BF16)
        rim[ch, 0:16, cols] = made[0:16]
        rim[ch, 16:32, cols] = made[OWNER_ROWS - 16:]
        return carry

    lax.fori_loop(0, 2 * per_channel, farther, 0)

    for j in range(2):
        remote(sblk.at[j], rblk.at[j], blk_s.at[j], blk_r.at[j], at(1)).wait_recv()
    row_in = lax.rem(row16, 8)
    ramp_rim = jnp.minimum(row_in + 1, 8 - row_in).astype(F32)
    inside = jnp.where(
        row_in < 4, jnp.where(me == n_tile - 1, 0.0, 1.0).astype(F32), jnp.where(me == 0, 0.0, 1.0).astype(F32)
    )
    inside = jnp.where(jnp.logical_or(row_in == 3, row_in == 4), 0.0, inside)
    beside_rows = []
    for i in range(reps):
        lanes = slice(i * 128, i * 128 + 128)
        below = jnp.concatenate([strip[2, 0, :, lanes], strip[2, 1, :, lanes]], axis=0)
        above = jnp.concatenate([strip[1, 0, :, lanes], strip[1, 1, :, lanes]], axis=0)
        rows = rblk[0, :, lanes].astype(F32) + rblk[1, :, lanes].astype(F32) + jnp.where(row_in < 4, below, above)
        if i == 0:
            weights = jnp.where(row_in < 4, rows[3:4], rows[4:5]) * ramp_rim
        beside_rows.append(rows.astype(BF16))
    rim_share = inside / jnp.maximum(weights, 1.0)

    def put_rim(d, lanes, v):
        vrim[d * TILE_ROWS:(d + 1) * TILE_ROWS, lanes] = v

    spread(beside_rows, rim_share, put_rim)
    for ch in range(2):
        for first in range(0, width, SPAN):
            cols = slice(first, first + SPAN)
            made = rim[ch, :, cols] + jnp.dot(mrim[ch], vrim[:, cols], preferred_element_type=F32)
            out_ref[0, ch, 0:16, cols] = made[0:16].astype(BF16)
            out_ref[0, ch, OWNER_ROWS - 16:, cols] = made[16:32].astype(BF16)

    for e in range(4):
        for k in range(2):
            send_tile(e, k, NEAR[e]).wait_send()
    for e in range(5):
        send_meta(e).wait_send()
    for copy in sends:
        copy.wait_send()

    @pl.when(inner)
    def _():
        for k in range(1, n_plane):
            remote(prof.at[core, plane], prof.at[core, plane], gat_s.at[k], gat_r.at[plane], mate(k)).wait_send()
        to_side.wait_send()
        pass_on.wait_send()


def solution(mesh):
    n_tile, n_plane = mesh.shape["tile"], mesh.shape["plane"]

    def per_device(raw_tiles, flat_profile, dark_profile, destinations, positions, levels):
        width = raw_tiles.shape[-1]
        tile = (2, TILE_ROWS, width)
        dma = pltpu.SemaphoreType.DMA
        return pl.pallas_call(
            functools.partial(stitch_kernel, n_tile, n_plane, width),
            out_shape=pltpu.VMEM((1, 2, OWNER_ROWS, width), BF16),
            in_specs=[pl.BlockSpec(memory_space=pltpu.HBM)] * 6,
            out_specs=pl.BlockSpec(memory_space=pltpu.VMEM),
            scratch_shapes=[
                pltpu.SMEM((1, 8), jnp.int32),
                pltpu.SMEM((1, 8), jnp.int32),
                pltpu.SMEM((1, 8), jnp.int32),
                pltpu.VMEM((8,) + tile, BF16),
                pltpu.VMEM((5, 2) + tile, BF16),
                pltpu.VMEM((6, 2) + tile, BF16),
                pltpu.VMEM((6, 8, 128), F32),
                pltpu.VMEM((6, 8, 128), F32),
                pltpu.VMEM((2, n_plane, 2, TILE_ROWS // n_plane, width), BF16),
                pltpu.VMEM(tile, F32),
                pltpu.VMEM(tile, F32),
                pltpu.VMEM((16, 128), F32),
                pltpu.VMEM((16, 128), F32),
                pltpu.VMEM((16, 128), F32),
                pltpu.VMEM((2, 2, 8, width), F32),
                pltpu.VMEM((4, 2, 8, width), F32),
                pltpu.VMEM((2, 16, width), BF16),
                pltpu.VMEM((2, 16, width), BF16),
                pltpu.VMEM(tile, BF16),
                pltpu.VMEM((12,) + tile, BF16),
                pltpu.VMEM((2, DEPTH, width), BF16),
                pltpu.VMEM((OWNER_ROWS, DEPTH), BF16),
                pltpu.VMEM((2, OWNER_ROWS, width), F32),
                pltpu.VMEM((2, 32, width), F32),
                pltpu.VMEM((64, width), BF16),
                pltpu.VMEM((2, 32, 64), BF16),
                dma, dma, dma((3,)), pltpu.SemaphoreType.REGULAR,
                dma((5, 2)), dma((5, 2)), dma((5,)), dma((5,)),
                dma((n_plane,)), dma((n_plane,)), dma, dma, dma, dma,
                dma((2,)), dma((2,)), dma, dma,
            ],
            compiler_params=pltpu.CompilerParams(
                collective_id=0, has_side_effects=True, vmem_limit_bytes=(62 << 20) - (64 << 10)
            ),
            name="stitch",
        )(destinations[:, :, 0], positions, levels, raw_tiles, flat_profile, dark_profile)

    placed = (
        P("plane", "tile", None, None, None),
        P(None, "plane", None),
        P(None, "plane", None),
        P("plane", "tile", None),
        P("plane", "tile"),
        P("plane", "tile"),
    )
    return jax.shard_map(
        per_device, mesh=mesh, in_specs=placed, out_specs=P("plane", None, "tile", None), check_vma=False
    )
```

```python
import functools

import jax
import jax.numpy as jnp
from jax import lax
from jax.experimental import pallas as pl
from jax.experimental.pallas import tpu as pltpu
from jax.sharding import PartitionSpec as P

MESH = pl.DeviceIdType.MESH
F32 = jnp.float32
BF16 = jnp.bfloat16
OWNER_ROWS = 512
TILE_ROWS = 16
NEAR = (-2, -1, 1, 2)
GROUPS = 6
DEPTH = GROUPS * 128
NEARER = 4 * 128
SPAN = 1024
Q = 1.0 / 4.5
Q2 = Q * Q
Q3 = Q2 * Q


def stitch_kernel(
    n_tile, n_plane, width,
    dest_hbm, pos_hbm, level_hbm, raw_ref, flat_ref, dark_ref, out_ref,
    dest_ref, pos_ref, level_ref,
    rawv, sbuf, rbuf, smeta, rmeta, prof, dark_v, inv_v, pos_all, gain_all, g_all,
    edge, strip, sblk, rblk, passing, wbuf, vbuf, mbuf, acc, rim, vrim, mrim,
    raw_sem, own_sem, int_sem, go_sem,
    tile_s, tile_r, meta_s, meta_r, gat_s, gat_r, side_s, side_r, swap_s, swap_r, blk_s, blk_r, pass_s, pass_r,
):
    me = lax.axis_index("tile")
    plane = lax.axis_index("plane")
    core = lax.rem(me, 2)
    column = lax.rem(me // 2, 4)
    up = column >= 2
    inner = jnp.logical_or(column == 1, column == 2)
    half = n_tile // 2
    reps = width // 128

    def at(offset):
        return {"tile": lax.rem(me + offset + n_tile, n_tile), "plane": plane}

    def mate(k):
        return {"tile": me, "plane": lax.rem(plane + k, n_plane)}

    def late_of(device):
        return lax.rem(device // 8, 2)

    is_late = late_of(me)
    late = is_late == 1
    early = is_late == 0
    outer = jnp.logical_not(inner)
    far = jnp.where(up, 3, 0)
    far_offset = jnp.where(up, 2, -2)
    next_far = jnp.where(up, 2, 1)
    next_crosses = core == jnp.where(up, 1, 0)
    crossing = jnp.where(next_crosses, 2, 1)

    def crosses(offset):
        return late_of(lax.rem(me + offset + n_tile, n_tile)) != is_late

    barrier = pltpu.get_barrier_semaphore()
    for offset in NEAR + (half,):
        @pl.when(jnp.logical_or(early, jnp.logical_not(crosses(offset))))
        def _():
            pl.semaphore_signal(barrier, inc=1, device_id=at(offset), device_id_type=MESH)

    @pl.when(inner)
    def _():
        for k in range(1, n_plane):
            pl.semaphore_signal(barrier, inc=1, device_id=mate(k), device_id_type=MESH)

    @pl.when(early)
    def _():
        pl.semaphore_signal(barrier, inc=1, device_id=at(2 * far_offset), device_id_type=MESH)

    loads = [
        pltpu.make_async_copy(src, dst, int_sem.at[j])
        for j, (src, dst) in enumerate(((dest_hbm, dest_ref), (pos_hbm, pos_ref), (level_hbm, level_ref)))
    ]
    for load in loads:
        load.start()
    load_raw = pltpu.make_async_copy(raw_ref.at[0], rawv, raw_sem)
    load_raw.start()

    @pl.when(jnp.logical_and(inner, core == 0))
    def _():
        pltpu.make_async_copy(flat_ref, prof.at[0, plane], own_sem).start()

    @pl.when(jnp.logical_and(inner, core == 1))
    def _():
        pltpu.make_async_copy(dark_ref, prof.at[1, plane], own_sem).start()

    for load in loads:
        load.wait()
    rel = [lax.rem(dest_ref[0, t] - me + 2 + 2 * n_tile, n_tile) for t in range(8)]
    picks = []
    for e, offset in enumerate(NEAR + (half, 0)):
        key = offset + 2
        first, last, hits = jnp.int32(0), jnp.int32(0), jnp.int32(0)
        for t in range(8):
            hit = rel[t] == key
            last = jnp.where(hit, t, last)
            hits = hits + jnp.where(hit, 1, 0)
            first = jnp.where(rel[7 - t] == key, 7 - t, first)
        gain0 = jnp.where(hits > 0, level_ref[0, first], 0).astype(F32)
        gain1 = jnp.where(hits > 1, level_ref[0, last], 0).astype(F32)
        pos0 = pos_ref[0, first].astype(F32)
        pos1 = pos_ref[0, last].astype(F32)
        row = lax.broadcasted_iota(jnp.int32, (8, 128), 0)
        meta = jnp.where(row == 0, pos0, jnp.where(row == 1, pos1, jnp.where(row == 2, gain0, gain1)))
        smeta[e] = meta
        if e == 5:
            rmeta[5] = meta
        picks.append((first, last))
    load_raw.wait()
    for e, (first, last) in enumerate(picks):
        if e == 5:
            rbuf[5, 0] = rawv[first]
            rbuf[5, 1] = rawv[last]
        else:
            sbuf[e, 0] = rawv[first]
            sbuf[e, 1] = rawv[last]

    @pl.when(inner)
    def _():
        pltpu.make_async_copy(flat_ref, prof.at[core, plane], own_sem).wait()

    pl.semaphore_wait(barrier, jnp.where(inner, 4 + n_plane + is_late, jnp.where(late, 6, 5 - crossing)))

    @pl.when(late)
    def _():
        for offset in NEAR:
            @pl.when(crosses(offset))
            def _():
                pl.semaphore_signal(go_sem, inc=1, device_id=at(offset), device_id_type=MESH)

    @pl.when(jnp.logical_and(late, outer))
    def _():
        pl.semaphore_signal(go_sem, inc=1, device_id=at(2 * far_offset), device_id_type=MESH)

    sends = []

    def remote(src, dst, s_sem, r_sem, device):
        return pltpu.make_async_remote_copy(src, dst, s_sem, r_sem, device_id=device, device_id_type=MESH)

    def send(src, dst, s_sem, r_sem, device):
        copy = remote(src, dst, s_sem, r_sem, device)
        copy.start()
        sends.append(copy)

    def slot_at_target(e):
        return 3 - e if e < 4 else 4

    def send_meta(e):
        f = slot_at_target(e)
        return remote(smeta.at[e], rmeta.at[f], meta_s.at[e], meta_r.at[f], at((NEAR + (half,))[e]))

    for e, offset in enumerate(NEAR + (half,)):
        @pl.when(jnp.logical_or(late, jnp.logical_not(crosses(offset))))
        def _():
            send_meta(e).start()

    @pl.when(inner)
    def _():
        for k in range(1, n_plane):
            remote(prof.at[core, plane], prof.at[core, plane], gat_s.at[k], gat_r.at[plane], mate(k)).start()

    def send_tile(e, k, offset):
        return remote(sbuf.at[e, k], rbuf.at[3 - e, k], tile_s.at[e, k], tile_r.at[3 - e, k], at(offset))

    def send_far():
        send_tile(far, 0, far_offset).start()

    def send_next():
        for k in range(2):
            send_tile(next_far, k, jnp.where(up, 1, -1)).start()

    def send_near():
        for j in range(2):
            e = jnp.where(up, j, 3 - j)
            for k in range(2):
                send_tile(e, k, jnp.where(up, j - 2, 2 - j)).start()

    @pl.when(jnp.logical_not(inner))
    def _():
        remote(sbuf.at[far, 1], passing, tile_s.at[far, 1], pass_r, at(-far_offset)).start()

    @pl.when(jnp.logical_and(outer, jnp.logical_or(late, jnp.logical_not(next_crosses))))
    def _():
        send_next()

    @pl.when(jnp.logical_and(outer, late))
    def _():
        send_far()

    for k in range(2):
        send(sbuf.at[4, k], rbuf.at[4, k], tile_s.at[4, k], tile_r.at[4, k], at(half))

    @pl.when(jnp.logical_not(inner))
    def _():
        send_near()

    to_side = remote(prof.at[core], prof.at[core], side_s, side_r, at(far_offset))
    pass_on = remote(passing, rbuf.at[3 - far, 1], pass_s, tile_r.at[3 - far, 1], at(2 * far_offset))
    def forward():
        remote(sbuf.at[far, 1], passing, tile_s.at[far, 1], pass_r, at(-far_offset)).wait_recv()
        pass_on.start()

    @pl.when(inner)
    def _():
        send_tile(far, 1, far_offset).start()
        send_far()
        send_next()

    @pl.when(jnp.logical_and(inner, late))
    def _():
        forward()

    @pl.when(inner)
    def _():
        for k in range(1, n_plane):
            source = lax.rem(plane + k, n_plane)
            remote(prof.at[core, source], prof.at[core, source], gat_s.at[k], gat_r.at[source], mate(k)).wait_recv()
        to_side.start()
        send_near()

    @pl.when(jnp.logical_and(early, outer))
    def _():
        pl.semaphore_wait(go_sem, crossing)
        for e, offset in enumerate(NEAR):
            @pl.when(crosses(offset))
            def _():
                send_meta(e).start()

        @pl.when(next_crosses)
        def _():
            send_next()

        send_far()

    @pl.when(jnp.logical_and(early, inner))
    def _():
        pl.semaphore_wait(go_sem, 1)
        forward()

    @pl.when(jnp.logical_not(inner))
    def _():
        to_side.wait_recv()

    other = {"tile": me + 1 - 2 * core, "plane": plane}
    send(prof.at[core], prof.at[core], swap_s, swap_r, other)

    row16 = lax.broadcasted_iota(jnp.int32, (TILE_ROWS, 128), 0)
    ramp = jnp.minimum(row16 + 1, TILE_ROWS - row16).astype(F32)
    lane = lax.broadcasted_iota(jnp.int32, (1, 128), 1)
    gap = lax.rem(lane // TILE_ROWS, 4).astype(F32)
    lane_row = lax.rem(lane, TILE_ROWS).astype(F32)
    lane16 = lax.broadcasted_iota(jnp.int32, (TILE_ROWS, 128), 1)
    lane_b = lane16.astype(F32).astype(BF16)

    def wide(x):
        return jnp.concatenate([x] * reps, axis=1)

    y32 = lax.broadcasted_iota(jnp.int32, (32, 128), 0)
    y32 = jnp.where(y32 < 16, y32, y32 + OWNER_ROWS - 32).astype(F32)
    rim_row = lax.rem(lane, 8).astype(F32)
    rim_row = jnp.where(rim_row < 4, rim_row + OWNER_ROWS, rim_row - 8.0)
    rim_hit = jnp.where(jnp.abs(y32 - rim_row) == gap, 1.0, 0.0)
    for ch in range(2):
        own = lax.rem(lane // 8, 2) == ch
        mrim[ch] = jnp.where(own, rim_hit, 0.0).astype(BF16)[:, 0:64]
    edge[...] = jnp.zeros(edge.shape, F32)
    pos_all[...] = jnp.full((16, 128), -99.0, F32)
    gain_all[...] = jnp.zeros((16, 128), F32)

    remote(prof.at[1 - core], prof.at[1 - core], swap_s, swap_r, other).wait_recv()
    part = TILE_ROWS // n_plane
    for p in range(n_plane):
        inv_v[:, p * part:(p + 1) * part, :] = 1.0 / prof[0, p].astype(F32)
        dark_v[:, p * part:(p + 1) * part, :] = prof[1, p].astype(F32)

    row_wide = lax.broadcasted_iota(jnp.int32, (TILE_ROWS, width), 0)
    gain_row = jnp.logical_or(row_wide == 3, row_wide == 12)
    gain_row16 = jnp.logical_or(row16 == 3, row16 == 12)

    for e in range(4):
        lo, at_pos = (8, 31.0) if e < 2 else (0, 0.0)
        for ch in range(2):
            total = None
            for k in range(2):
                keep = jnp.where(smeta[e, k:k + 1, :] == at_pos, 1.0, 0.0)
                scale = wide(ramp[lo:lo + 8] * smeta[e, 2 + k:3 + k, :])
                tile = sbuf[e, k, ch].astype(F32)[lo:lo + 8]
                w = (tile - dark_v[ch, lo:lo + 8]) * inv_v[ch, lo:lo + 8] * scale
                w = jnp.where(gain_row[lo:lo + 8], wide(smeta[e, 2 + k:3 + k, :]), w.astype(BF16).astype(F32))
                w = w * wide(jnp.broadcast_to(keep, (8, 128)))
                total = w if total is None else total + w
            strip[e, ch] = total
    order = (5, 4) + tuple(jnp.where(up, a, 3 - a) for a in (1, 0, 2, 3))

    def take_meta(m):
        if m > 0:
            f = order[m]
            remote(smeta.at[0], rmeta.at[f], meta_s.at[0], meta_r.at[f], at(1)).wait_recv()
        pos_all[2 * m:2 * m + 2] = rmeta[order[m], 0:2]
        gain_all[2 * m:2 * m + 2] = rmeta[order[m], 2:4]

    for m in range(4):
        take_meta(m)

    y = lax.broadcasted_iota(jnp.int32, (OWNER_ROWS, 128), 0).astype(F32)
    y16 = lax.broadcasted_iota(jnp.int32, (16, 128), 0).astype(F32)
    top_shift = jnp.where(me == 0, 2.0, 1e6).astype(F32)
    bottom_shift = jnp.where(me == n_tile - 1, -1.0 * OWNER_ROWS - 16.0, 1e6).astype(F32)

    def place(m):
        p0, p1 = pos_all[2 * m:2 * m + 1], pos_all[2 * m + 1:2 * m + 2]
        source_row = jnp.where(lane < 64, p0, p1) * TILE_ROWS + lane_row
        cols = slice(m * 128, (m + 1) * 128)

        def hits(d):
            return jnp.where(jnp.abs(d) == gap, 1.0, 0.0)

        mbuf[:, cols] = hits(y - source_row).astype(BF16)
        mbuf[0:16, cols] = (hits(y16 - source_row) - hits(y16 + source_row + top_shift)).astype(BF16)
        low = OWNER_ROWS - 16.0
        mbuf[OWNER_ROWS - 16:, cols] = (
            hits(y16 + low - source_row) - hits(y16 + source_row + bottom_shift)
        ).astype(BF16)

    def spread(pieces, share, put):
        nothing = jnp.zeros((TILE_ROWS, 128), BF16)
        right, left = {}, {}
        for d in (1, 2, 3):
            right[d] = [pltpu.roll(x, d, 1) for x in pieces]
            left[d] = [pltpu.roll(x, 128 - d, 1) for x in pieces]
        for i in range(reps):
            x = pieces[i].astype(F32)
            s = {}
            for d in (1, 2, 3):
                r = jnp.where(lane_b < d, right[d][i - 1] if i else nothing, right[d][i]).astype(F32)
                l = jnp.where(lane_b >= 128 - d, left[d][i + 1] if i + 1 < reps else nothing, left[d][i]).astype(F32)
                s[d] = r + l
                if d == 1:
                    r1, l1 = r, l
            second, third = s[2], s[3]
            if i == 0:
                second = second - jnp.where(lane16 == 0, x, 0.0)
                third = third - jnp.where(lane16 == 0, l1, jnp.where(lane16 == 1, r1, 0.0))
            if i == reps - 1:
                second = second - jnp.where(lane16 == 127, x, 0.0)
                third = third - jnp.where(lane16 == 127, r1, jnp.where(lane16 == 126, l1, 0.0))
            zero = (0.5 * Q + 2.0 * Q3) * x + (0.5 * Q2 + 9.0 * Q3) * s[1] + (0.5 * Q3) * second + Q3 * third
            one = (0.5 * Q2 + 9.0 * Q3) * x + Q3 * s[1] + (3.0 * Q3) * second
            two = (0.5 * Q3) * x + (3.0 * Q3) * s[1]
            for d, v in enumerate((zero, one, two, Q3 * x)):
                put(d, slice(i * 128, i * 128 + 128), (v * share).astype(BF16))

    last_row = jnp.where(up, 31.0, 0.0).astype(F32)
    other_row = jnp.where(up, 0.0, 31.0).astype(F32)

    def weigh(m, k):
        e = order[m]
        if m > 0:
            remote(sbuf.at[0, k], rbuf.at[e, k], tile_s.at[0, k], tile_r.at[e, k], at(1)).wait_recv()
        j = 2 * m + k
        p = pos_all[j:j + 1]
        keep_near = jnp.broadcast_to(jnp.where(p == last_row, 1.0, 0.0), (8, 128))
        keep_far = jnp.broadcast_to(jnp.where(p == other_row, 1.0, 0.0), (8, 128))
        scale = ramp * gain_all[j:j + 1]

        def unit(ch, carry):
            for i in range(reps):
                lanes = slice(i * 128, i * 128 + 128)
                w = (rbuf[e, k, ch, :, lanes].astype(F32) - dark_v[ch, :, lanes]) * inv_v[ch, :, lanes] * scale
                w = w.astype(BF16)
                wbuf[j, ch, :, lanes] = w
                w = jnp.where(gain_row16, gain_all[j:j + 1], w.astype(F32))
                if m < 4:
                    edge[0, ch, :, lanes] += keep_near * jnp.where(up, w[8:16], w[0:8])
                if m < 2 or m >= 4:
                    edge[1, ch, :, lanes] += keep_far * jnp.where(up, w[0:8], w[8:16])
            return carry

        lax.fori_loop(0, 2, unit, 0)

    def filter_columns(m, k):
        j = 2 * m + k
        share = 1.0 / jnp.maximum(ramp * g_all[j:j + 1], 1.0)

        def unit(ch, carry):
            def put(d, lanes, v):
                start = m * 128 + k * 64 + d * TILE_ROWS
                vbuf[ch, start:start + TILE_ROWS, lanes] = v

            spread([wbuf[j, ch, :, i * 128:i * 128 + 128] for i in range(reps)], share, put)
            return carry

        lax.fori_loop(0, 2, unit, 0, unroll=True)

    def send_edge(j):
        down = up if j == 0 else jnp.logical_not(up)
        row8 = lax.broadcasted_iota(jnp.int32, (8, width), 0)
        block = []
        for ch in range(2):
            sums, ours = edge[j, ch], jnp.where(down, strip[3, ch], strip[0, ch])
            below = jnp.where(down, ours, sums)
            above = jnp.where(down, sums, ours)
            block.append(jnp.where(row8 < 4, below, above))
        sblk[j] = jnp.concatenate(block, axis=0).astype(BF16)
        offset = jnp.where(down, 1, -1)
        lands = jnp.where(down, 0, 1)
        send(sblk.at[j], rblk.at[lands], blk_s.at[j], blk_r.at[lands], at(offset))

    for m in range(4):
        place(m)
    for m in range(4):
        for k in range(2):
            weigh(m, k)

    send_edge(0)
    for m in range(4, GROUPS):
        take_meta(m)
    positions, gains = pos_all[...], gain_all[...]
    for j in range(12):
        own = jnp.where(positions == positions[j:j + 1], gains, 0.0)
        g_all[j:j + 1] = jnp.sum(own, axis=0, keepdims=True)
    for m in range(4, GROUPS):
        place(m)
    for m in range(4):
        for k in range(2):
            filter_columns(m, k)

    per_channel = width // SPAN

    def chunk(n):
        return n // per_channel, pl.ds(pl.multiple_of(lax.rem(n, per_channel) * SPAN, SPAN), SPAN)


    for k in range(2):
        for m in range(4, GROUPS):
            weigh(m, k)
    send_edge(1)
    for k in range(2):
        for m in range(4, GROUPS):
            filter_columns(m, k)

    def farther(n, carry):
        ch, cols = chunk(n)
        made = jnp.dot(mbuf[...], vbuf[ch, :, cols], preferred_element_type=F32)
        out_ref[0, ch, :, cols] = made.astype(BF16)
        rim[ch, 0:16, cols] = made[0:16]
        rim[ch, 16:32, cols] = made[OWNER_ROWS - 16:]
        return carry

    lax.fori_loop(0, 2 * per_channel, farther, 0)

    for j in range(2):
        remote(sblk.at[j], rblk.at[j], blk_s.at[j], blk_r.at[j], at(1)).wait_recv()
    row_in = lax.rem(row16, 8)
    ramp_rim = jnp.minimum(row_in + 1, 8 - row_in).astype(F32)
    inside = jnp.where(
        row_in < 4, jnp.where(me == n_tile - 1, 0.0, 1.0).astype(F32), jnp.where(me == 0, 0.0, 1.0).astype(F32)
    )
    inside = jnp.where(jnp.logical_or(row_in == 3, row_in == 4), 0.0, inside)
    beside_rows = []
    for i in range(reps):
        lanes = slice(i * 128, i * 128 + 128)
        below = jnp.concatenate([strip[2, 0, :, lanes], strip[2, 1, :, lanes]], axis=0)
        above = jnp.concatenate([strip[1, 0, :, lanes], strip[1, 1, :, lanes]], axis=0)
        rows = rblk[0, :, lanes].astype(F32) + rblk[1, :, lanes].astype(F32) + jnp.where(row_in < 4, below, above)
        if i == 0:
            weights = jnp.where(row_in < 4, rows[3:4], rows[4:5]) * ramp_rim
        beside_rows.append(rows.astype(BF16))
    rim_share = inside / jnp.maximum(weights, 1.0)

    def put_rim(d, lanes, v):
        vrim[d * TILE_ROWS:(d + 1) * TILE_ROWS, lanes] = v

    spread(beside_rows, rim_share, put_rim)
    for ch in range(2):
        for first in range(0, width, SPAN):
            cols = slice(first, first + SPAN)
            made = rim[ch, :, cols] + jnp.dot(mrim[ch], vrim[:, cols], preferred_element_type=F32)
            out_ref[0, ch, 0:16, cols] = made[0:16].astype(BF16)
            out_ref[0, ch, OWNER_ROWS - 16:, cols] = made[16:32].astype(BF16)

    for e in range(4):
        for k in range(2):
            send_tile(e, k, NEAR[e]).wait_send()
    for e in range(5):
        send_meta(e).wait_send()
    for copy in sends:
        copy.wait_send()

    @pl.when(inner)
    def _():
        for k in range(1, n_plane):
            remote(prof.at[core, plane], prof.at[core, plane], gat_s.at[k], gat_r.at[plane], mate(k)).wait_send()
        to_side.wait_send()
        pass_on.wait_send()


def solution(mesh):
    n_tile, n_plane = mesh.shape["tile"], mesh.shape["plane"]

    def per_device(raw_tiles, flat_profile, dark_profile, destinations, positions, levels):
        width = raw_tiles.shape[-1]
        tile = (2, TILE_ROWS, width)
        dma = pltpu.SemaphoreType.DMA
        return pl.pallas_call(
            functools.partial(stitch_kernel, n_tile, n_plane, width),
            out_shape=pltpu.VMEM((1, 2, OWNER_ROWS, width), BF16),
            in_specs=[pl.BlockSpec(memory_space=pltpu.HBM)] * 6,
            out_specs=pl.BlockSpec(memory_space=pltpu.VMEM),
            scratch_shapes=[
                pltpu.SMEM((1, 8), jnp.int32),
                pltpu.SMEM((1, 8), jnp.int32),
                pltpu.SMEM((1, 8), jnp.int32),
                pltpu.VMEM((8,) + tile, BF16),
                pltpu.VMEM((5, 2) + tile, BF16),
                pltpu.VMEM((6, 2) + tile, BF16),
                pltpu.VMEM((6, 8, 128), F32),
                pltpu.VMEM((6, 8, 128), F32),
                pltpu.VMEM((2, n_plane, 2, TILE_ROWS // n_plane, width), BF16),
                pltpu.VMEM(tile, F32),
                pltpu.VMEM(tile, F32),
                pltpu.VMEM((16, 128), F32),
                pltpu.VMEM((16, 128), F32),
                pltpu.VMEM((16, 128), F32),
                pltpu.VMEM((2, 2, 8, width), F32),
                pltpu.VMEM((4, 2, 8, width), F32),
                pltpu.VMEM((2, 16, width), BF16),
                pltpu.VMEM((2, 16, width), BF16),
                pltpu.VMEM(tile, BF16),
                pltpu.VMEM((12,) + tile, BF16),
                pltpu.VMEM((2, DEPTH, width), BF16),
                pltpu.VMEM((OWNER_ROWS, DEPTH), BF16),
                pltpu.VMEM((2, OWNER_ROWS, width), F32),
                pltpu.VMEM((2, 32, width), F32),
                pltpu.VMEM((64, width), BF16),
                pltpu.VMEM((2, 32, 64), BF16),
                dma, dma, dma((3,)), pltpu.SemaphoreType.REGULAR,
                dma((5, 2)), dma((5, 2)), dma((5,)), dma((5,)),
                dma((n_plane,)), dma((n_plane,)), dma, dma, dma, dma,
                dma((2,)), dma((2,)), dma, dma,
            ],
            compiler_params=pltpu.CompilerParams(
                collective_id=0, has_side_effects=True, vmem_limit_bytes=(62 << 20) - (64 << 10)
            ),
            name="stitch",
        )(destinations[:, :, 0], positions, levels, raw_tiles, flat_profile, dark_profile)

    placed = (
        P("plane", "tile", None, None, None),
        P(None, "plane", None),
        P(None, "plane", None),
        P("plane", "tile", None),
        P("plane", "tile"),
        P("plane", "tile"),
    )
    return jax.shard_map(
        per_device, mesh=mesh, in_specs=placed, out_specs=P("plane", None, "tile", None), check_vma=False
    )
```
